32 devices in a mesh: seq: 4 (over z), tp: 8 (over y, x, core).
Axes of the slice: x: 2, y: 2, z: 4, core: 2. Of those that a mesh axis runs over, the one named last changes fastest.
Arguments:
- tokens: bfloat16 [1024, 6144], P(('seq', 'tp')), may hold values from -6 to 6
- proj_weight: bfloat16 [6144, 4, 4096], P(None, None, 'tp'), may hold values from -0.078125 to 0.078125
- out_weight: bfloat16 [4096, 6144], P('tp'), may hold values from -0.09375 to 0.09375
- head_gain: float32 [4096], P('tp'), may hold values from 0.1 to 1.9
- decay_rate: float32 [32], P('tp'), as said below
Outputs:
- layer_out: bfloat16 [1024, 6144], P(('seq', 'tp'))
The draws below stay inside these ranges and needn't reach their ends.
Inputs may be any that keep to these rules, and one draw needn't show every extreme that they name: `decay_rate`: every rate is positive.
All inputs are finite; a program needn't handle non-finite values.
Results may differ from the reference program's by a relative error of at most 0.015.
Values may be sent and summed in bfloat16 or wider, within the bound.
No kernel may reach another device: no remote copies, remote signals or barrier semaphores. Data moves between devices by JAX's collectives and lax.ppermute only.
A program may use at most 128 MiB of HBM per device.

```python
import jax
import jax.numpy as jnp
from jax import lax

D = 6144
HEADS = 32
HD = 128
BLOCK = 256
TOKENS = 1024
N_TP = 8


def draw_decay_rate(key, part):
    key_mask, key_slow, key_fast = jax.random.split(key, 3)
    share = 0.5
    slow_heads = jax.random.uniform(key_mask, (HEADS,), jnp.float32) < share
    slow = jax.random.uniform(key_slow, (HEADS,), jnp.float32, 0.1, 2.0) / TOKENS
    fast = jnp.exp(jax.random.uniform(key_fast, (HEADS,), jnp.float32, jnp.log(1.0 / 500.0), jnp.log(1.0 / 30.0)))
    return jnp.where(slow_heads, slow, fast).astype(jnp.float32)


def shard_levels(key, dims, shards, least, high):
    def one(axis_at, shards_of):
        draws = jax.random.uniform(jax.random.fold_in(jax.random.fold_in(key, 6), axis_at), (shards_of,), jnp.float32, least / len(shards), high / len(shards))
        return jnp.repeat(jnp.exp(draws), dims[axis_at] // shards_of).reshape((-1,) + (1,) * (len(dims) - axis_at - 1))

    factor_of = one(*shards[0])
    for cut in shards[1:]:
        factor_of = factor_of * one(*cut)
    return factor_of


def normal_values(key, shape, spread, limit, shards=(), dtype=jnp.bfloat16):
    drawn = spread * jax.random.normal(key, shape, jnp.float32)
    if shards:
        drawn = drawn * shard_levels(key, shape, shards, -0.22, 0.18)
    return jnp.clip(drawn, -limit, limit).astype(dtype)


def setup_inputs(seed: int = 0) -> dict:
    key_list = jax.random.split(jax.random.key(seed), 6)
    return {
        "tokens": normal_values(key_list[0], (TOKENS, D), 1.0, 6.0, ((0, 32),)),
        "proj_weight": normal_values(key_list[1], (D, 4, HEADS * HD), D ** -0.5, 0.078125, ((2, 8),)),
        "out_weight": normal_values(key_list[2], (HEADS * HD, D), (HEADS * HD) ** -0.5, 0.09375, ((0, 8),)),
        "head_gain": jnp.clip(1.0 + 0.18 * jax.random.normal(key_list[3], (HEADS * HD,), jnp.float32), 0.1, 1.9),
        "decay_rate": draw_decay_rate(jax.random.fold_in(key_list[5], 71), 0),
    }


def attend(q_head, k_head, v_head, rate, start_state):
    count = q_head.shape[0] // BLOCK
    place = jnp.arange(BLOCK).astype(jnp.float32)
    diff = place[:, None] - place[None, :]
    causal = jnp.where(diff >= 0, jnp.exp(-rate * jnp.maximum(diff, 0.0)), 0.0)
    in_decay = jnp.exp(-rate * (place + 1.0))
    out_decay = jnp.exp(-rate * (BLOCK - 1.0 - place))
    block_decay = jnp.exp(-rate * BLOCK)
    q_blocks = q_head.reshape(count, BLOCK, q_head.shape[1])
    k_blocks = k_head.reshape(count, BLOCK, k_head.shape[1])
    v_blocks = v_head.reshape(count, BLOCK, v_head.shape[1])

    def advance(state, block):
        q_blk, k_blk, v_blk = block
        scores = jnp.dot(q_blk, k_blk.T, preferred_element_type=jnp.float32)
        weighted = (scores * causal).astype(jnp.bfloat16)
        inner = jnp.dot(weighted, v_blk, preferred_element_type=jnp.float32)
        carried = jnp.dot(q_blk.astype(jnp.float32), state, precision=lax.Precision.HIGHEST) * in_decay[:, None]
        scaled = k_blk.astype(jnp.float32) * out_decay[:, None]
        update = jnp.dot(scaled.T, v_blk.astype(jnp.float32), precision=lax.Precision.HIGHEST)
        return (block_decay * state + update, inner + carried)
    final_state, outputs = lax.scan(advance, start_state, (q_blocks, k_blocks, v_blocks))
    return (outputs.reshape(q_head.shape[0], q_head.shape[1]), final_state)

def finish(attn, gain, gate):
    square = lax.optimization_barrier(jnp.mean(attn * attn, axis=-1, keepdims=True))
    return attn * lax.rsqrt(square + 1e-06) * gain * jax.nn.sigmoid(gate)

def reference(tokens, proj_weight, out_weight, head_gain, decay_rate):

    def one_head(index):
        cols = lax.dynamic_slice_in_dim(proj_weight, index * HD, HD, 2).reshape(D, 4 * HD)
        mixed = jnp.dot(tokens, cols, preferred_element_type=jnp.float32)
        q_head = jax.nn.silu(mixed[:, :HD]).astype(jnp.bfloat16)
        k_head = jax.nn.silu(mixed[:, HD:2 * HD]).astype(jnp.bfloat16)
        v_head = jax.nn.silu(mixed[:, 2 * HD:3 * HD]).astype(jnp.bfloat16)
        rate = lax.dynamic_slice_in_dim(decay_rate, index, 1, 0)[0]
        gain = lax.dynamic_slice_in_dim(head_gain, index * HD, HD, 0)
        attn, unused = attend(q_head, k_head, v_head, rate, jnp.zeros((HD, HD), jnp.float32))
        return finish(attn, gain[None, :], mixed[:, 3 * HD:]).astype(jnp.bfloat16)
    heads_out = lax.map(one_head, jnp.arange(HEADS).astype(jnp.int32))
    joined = jnp.transpose(heads_out, (1, 0, 2)).reshape(TOKENS, HEADS * HD)
    group = HEADS * HD // N_TP

    def add_group(total, index):
        part_y = lax.dynamic_slice_in_dim(joined, index * group, group, 1)
        part_w = lax.dynamic_slice_in_dim(out_weight, index * group, group, 0)
        partial_sum = jnp.dot(part_y, part_w, preferred_element_type=jnp.float32).astype(jnp.bfloat16)
        partial_sum = lax.optimization_barrier(partial_sum)
        return (total + partial_sum.astype(jnp.float32), None)
    total, unused = lax.scan(add_group, jnp.zeros((TOKENS, D), jnp.float32), jnp.arange(N_TP).astype(jnp.int32))
    return total.astype(jnp.bfloat16)
```

```python
import functools

import jax
import jax.numpy as jnp
from jax import lax
from jax.experimental import pallas as pl
from jax.experimental.pallas import tpu as pltpu
from jax.sharding import PartitionSpec as P

HD = 128
BLOCK = 256
F32, BF16 = jnp.float32, jnp.bfloat16
VMEM = pl.BlockSpec(memory_space=pltpu.VMEM)
SMEM = pl.BlockSpec(memory_space=pltpu.SMEM)
HBM = pl.BlockSpec(memory_space=pl.ANY)
MIB = 1 << 20


def entering(value, axis, combine, identity):
    count, position = (lax.axis_size(axis), lax.axis_index(axis))
    everything = jax.tree.map(
        lambda part, kind: lax.all_gather(part.astype(kind), axis),
        value,
        (jnp.bfloat16, jnp.bfloat16),
    )
    start = jax.tree.map(
        lambda part, zero: jnp.broadcast_to(jnp.asarray(zero, part.dtype), part.shape),
        value,
        identity,
    )

    def turn(k, before):
        reached = k < position
        new = combine(
            before, jax.tree.map(lambda part, own: part[k].astype(own.dtype), everything, value)
        )
        return jax.tree.map(lambda a, b: jnp.where(reached, a, b), new, before)

    return lax.fori_loop(0, count, turn, start)


def attend(q_head, k_head, v_head, rate, start_state):
    count = q_head.shape[0] // BLOCK
    place = jnp.arange(BLOCK).astype(jnp.float32)
    diff = place[:, None] - place[None, :]
    causal = jnp.where(diff >= 0, jnp.exp(-rate * jnp.maximum(diff, 0.0)), 0.0)
    in_decay = jnp.exp(-rate * (place + 1.0))
    out_decay = jnp.exp(-rate * (BLOCK - 1.0 - place))
    block_decay = jnp.exp(-rate * BLOCK)
    q_blocks = q_head.reshape(count, BLOCK, q_head.shape[1])
    k_blocks = k_head.reshape(count, BLOCK, k_head.shape[1])
    v_blocks = v_head.reshape(count, BLOCK, v_head.shape[1])

    def advance(state, block):
        q_blk, k_blk, v_blk = block
        scores = jnp.dot(q_blk, k_blk.T, preferred_element_type=jnp.float32)
        weighted = (scores * causal).astype(jnp.bfloat16)
        inner = jnp.dot(weighted, v_blk, preferred_element_type=jnp.float32)
        carried = (
            jnp.dot(q_blk.astype(jnp.float32), state, precision=lax.Precision.HIGHEST)
            * in_decay[:, None]
        )
        scaled = k_blk.astype(jnp.float32) * out_decay[:, None]
        update = jnp.dot(scaled.T, v_blk.astype(jnp.float32), precision=lax.Precision.HIGHEST)
        return (block_decay * state + update, inner + carried)

    final_state, outputs = lax.scan(advance, start_state, (q_blocks, k_blocks, v_blocks))
    return (outputs.reshape(q_head.shape[0], q_head.shape[1]), final_state)


def general_device(tokens, proj_weight, out_weight, head_gain, decay_rate):
    heads_here = decay_rate.shape[0]
    width = head_gain.shape[0]
    flat = proj_weight.reshape(proj_weight.shape[0], 4 * width)
    mixed = jnp.dot(
        lax.all_gather(tokens, "tp", axis=0, tiled=True), flat, preferred_element_type=jnp.float32
    )
    local_rows = mixed.shape[0]
    q_all = jax.nn.silu(mixed[:, :width]).astype(jnp.bfloat16).reshape(local_rows, heads_here, HD)
    k_all = (
        jax.nn.silu(mixed[:, width : 2 * width])
        .astype(jnp.bfloat16)
        .reshape(local_rows, heads_here, HD)
    )
    v_all = (
        jax.nn.silu(mixed[:, 2 * width : 3 * width])
        .astype(jnp.bfloat16)
        .reshape(local_rows, heads_here, HD)
    )
    gate = mixed[:, 3 * width :].reshape(local_rows, heads_here, HD)
    zero_state = jnp.zeros((HD, HD), jnp.float32)
    outputs, local_states = jax.vmap(attend, in_axes=(1, 1, 1, 0, None), out_axes=(1, 0))(
        q_all, k_all, v_all, decay_rate, zero_state
    )
    zero_states = jnp.zeros((heads_here, HD, HD), jnp.float32)
    span_decay = jnp.exp(-decay_rate * local_rows)

    def combine(earlier, later):
        return (later[1][:, None, None] * earlier[0] + later[0], earlier[1] * later[1])

    incoming, unused = entering(
        (local_states, span_decay), "seq", combine, (zero_states, jnp.ones_like(span_decay))
    )
    place = jnp.arange(local_rows).astype(jnp.float32)
    lift = jnp.exp(-decay_rate[None, :] * (place[:, None] + 1.0))
    extra = jnp.einsum(
        "thd,hde->the", q_all.astype(jnp.float32), incoming, precision=lax.Precision.HIGHEST
    )
    attn = outputs + extra * lift[:, :, None]
    square = jnp.mean(attn * attn, axis=-1, keepdims=True)
    normed = (
        attn
        * lax.rsqrt(square + 1e-06)
        * head_gain.reshape(heads_here, HD)[None]
        * jax.nn.sigmoid(gate)
    )
    joined = normed.astype(jnp.bfloat16).reshape(local_rows, width)
    return lax.psum_scatter(
        jnp.dot(joined, out_weight, preferred_element_type=jnp.float32).astype(jnp.bfloat16),
        "tp",
        scatter_dimension=0,
        tiled=True,
    )


CORE = [(i, i ^ 1) for i in range(8)]
FIRST = [(i, i ^ (4 if i & 1 else 2)) for i in range(8)]
SECOND = [(i, i ^ (2 if i & 1 else 4)) for i in range(8)]


def hop(value, pairs):
    return lax.ppermute(value, "tp", pairs)


STEP = 256


def pinned(value):
    return pltpu.with_memory_space_constraint(value, pltpu.VMEM)


def in_hbm(value):
    return pltpu.with_memory_space_constraint(value, pltpu.HBM)


def chunks_kernel(first, w_hbm, buf, sem):
    step = buf.shape[1]
    copies = [
        pltpu.make_async_copy(w_hbm.at[pl.ds(first + i * step, step)], buf.at[i], sem.at[i])
        for i in range(buf.shape[0])
    ]
    for copy in copies:
        copy.start()
    return copies


def turn(block, at, kv_ref, qg_ref):
    width = block.shape[2]
    turned = jnp.swapaxes(block, 0, 1)
    kv_ref[at, :width] = turned[1]
    kv_ref[at, width:] = turned[2]
    qg_ref[at, :width] = turned[0]
    qg_ref[at, width:] = turned[3]
    return turned


def slot_places(index, shape, axis):
    row = lax.broadcasted_iota(jnp.int32, shape, axis)
    part = shape[axis] // 8
    core = index & 1
    near = jnp.where(core == 0, 2, 4)
    far = 6 - near
    owners = (
        index,
        index ^ 1,
        index ^ near,
        index ^ 1 ^ far,
        index ^ far,
        index ^ 1 ^ near,
        index ^ 6,
        index ^ 7,
    )
    place = row
    for slot, owner in enumerate(owners):
        place = jnp.where(row // part == slot, row + (owner - slot) * part, place)
    return place.astype(F32)


def prep_kernel(w_hbm, kv_ref, qg_ref, down_ref, across_ref, buf, sem):
    step = buf.shape[1]
    copies = chunks_kernel(0, w_hbm, buf, sem)
    index = lax.axis_index("tp")
    down_ref[...] = slot_places(index, down_ref.shape, 0)
    across_ref[...] = slot_places(index, across_ref.shape, 1)
    for i, copy in enumerate(copies):
        copy.wait()
        turn(buf[i], slice(i * step, (i + 1) * step), kv_ref, qg_ref)


def prep(proj_weight, rows):
    depth, kinds, width = proj_weight.shape
    depth //= 2
    out = pltpu.VMEM((depth, 2 * width), BF16)
    return pl.pallas_call(
        prep_kernel,
        in_specs=[HBM],
        out_specs=[VMEM] * 4,
        out_shape=[out, out, pltpu.VMEM((rows, 1), F32), pltpu.VMEM((1, rows), F32)],
        scratch_shapes=[
            pltpu.VMEM((depth // STEP, STEP, kinds, width), BF16),
            pltpu.SemaphoreType.DMA((depth // STEP,)),
        ],
        compiler_params=pltpu.CompilerParams(vmem_limit_bytes=16 * MIB),
        cost_estimate=pl.CostEstimate(
            flops=0, bytes_accessed=2 * depth * kinds * width, transcendentals=0
        ),
        name="prep",
    )(in_hbm(proj_weight))


def gather_rows(x_refs, x_all):
    at = 0
    for ref in x_refs:
        x_all[at : at + ref.shape[0], :] = ref[...]
        at += ref.shape[0]


def silu(mixed):
    return (mixed / (1.0 + jnp.exp(-mixed))).astype(BF16)


def near_kernel(n_rows, *refs):
    x_refs = refs[:n_rows]
    kv0, qg0, w_hbm, kv1, qg1, k_ref, v_ref, q_ref, g_ref, x_all, total, buf, sem = refs[n_rows:]
    depth, step, width = kv0.shape[0], buf.shape[1], k_ref.shape[1]
    copies = chunks_kernel(depth, w_hbm, buf, sem)
    gather_rows(x_refs, x_all)
    for i, (ref, half) in enumerate(((qg0, 0), (kv0, 0), (kv0, 1), (qg0, 1))):
        total[i] = jnp.dot(
            x_all[:, :depth],
            ref[:, half * width : (half + 1) * width],
            preferred_element_type=F32,
        )
    for c, copy in enumerate(copies):
        copy.wait()
        turned = turn(buf[c], slice(c * step, (c + 1) * step), kv1, qg1)
        x = x_all[:, depth + c * step : depth + (c + 1) * step]
        for i in range(4):
            total[i] += jnp.dot(x, turned[i], preferred_element_type=F32)
    q_ref[...] = silu(total[0])
    k_ref[...] = silu(total[1])
    v_ref[...] = silu(total[2])
    g_ref[...] = 1.0 / (1.0 + jnp.exp(-total[3]))


def project_near(rows, kv0, qg0, proj_weight):
    count = sum(r.shape[0] for r in rows)
    depth, kinds, width = proj_weight.shape
    turned = pltpu.VMEM((depth // 2, 2 * width), BF16)
    half, wide = pltpu.VMEM((count, width), BF16), pltpu.VMEM((count, width), F32)
    chunks = depth // 2 // STEP
    return pl.pallas_call(
        functools.partial(near_kernel, len(rows)),
        in_specs=[VMEM] * (len(rows) + 2) + [HBM],
        out_specs=[VMEM] * 6,
        out_shape=[turned, turned, half, half, half, wide],
        scratch_shapes=[
            pltpu.VMEM((count, depth), BF16),
            pltpu.VMEM((kinds, count, width), F32),
            pltpu.VMEM((chunks, STEP, kinds, width), BF16),
            pltpu.SemaphoreType.DMA((chunks,)),
        ],
        compiler_params=pltpu.CompilerParams(vmem_limit_bytes=24 * MIB),
        cost_estimate=pl.CostEstimate(
            flops=2 * count * depth * kinds * width,
            bytes_accessed=depth * kinds * width,
            transcendentals=0,
        ),
        name="project_near",
    )(*rows, pinned(kv0), pinned(qg0), in_hbm(proj_weight))


def far_kernel(n_rows, gate, *refs):
    x_refs = refs[:n_rows]
    w0, w1, a_ref, b_ref, x_all = refs[n_rows:]
    depth, width = w0.shape[0], a_ref.shape[1]
    gather_rows(x_refs, x_all)
    for half, out in enumerate((a_ref, b_ref)):
        cols = slice(half * width, (half + 1) * width)
        mixed = jnp.dot(x_all[:, :depth], w0[:, cols], preferred_element_type=F32) + jnp.dot(
            x_all[:, depth:], w1[:, cols], preferred_element_type=F32
        )
        out[...] = 1.0 / (1.0 + jnp.exp(-mixed)) if gate and half else silu(mixed)


def project_far(rows, w0, w1, gate, name):
    count = sum(r.shape[0] for r in rows)
    depth, width = rows[0].shape[1], w0.shape[1] // 2
    return pl.pallas_call(
        functools.partial(far_kernel, len(rows), gate),
        in_specs=[VMEM] * (len(rows) + 2),
        out_specs=[VMEM] * 2,
        out_shape=[
            pltpu.VMEM((count, width), BF16),
            pltpu.VMEM((count, width), F32 if gate else BF16),
        ],
        scratch_shapes=[pltpu.VMEM((count, depth), BF16)],
        compiler_params=pltpu.CompilerParams(vmem_limit_bytes=12 * MIB),
        cost_estimate=pl.CostEstimate(
            flops=4 * count * depth * width, bytes_accessed=4 * depth * width, transcendentals=0
        ),
        name=name,
    )(*rows, pinned(w0), pinned(w1))


def state_kernel(rate_ref, place_ref, k0, k1, v0, v1, s_ref):
    for h in range(s_ref.shape[0]):
        cols = slice(h * HD, (h + 1) * HD)
        fade = jnp.exp(-rate_ref[h] * (BLOCK - 1.0 - place_ref[...]))
        k = jnp.concatenate([k0[:, cols], k1[:, cols]], 0).astype(F32) * fade
        v = jnp.concatenate([v0[:, cols], v1[:, cols]], 0)
        s_ref[h] = lax.dot_general(
            k.astype(BF16), v, (((0,), (0,)), ((), ())), preferred_element_type=F32
        ).astype(BF16)


def middle_kernel(n_rows, rate_ref, place_ref, across_ref, *refs):
    x_refs = refs[:n_rows]
    (w0, w1, q0, k0, k1, v0, v1, w_hbm, u_hbm) = refs[n_rows : n_rows + 9]
    (q1, g1, o_ref, w_ref, u_ref, x_all, sem) = refs[n_rows + 9 :]
    copies = [
        pltpu.make_async_copy(w_hbm, w_ref, sem.at[0]),
        pltpu.make_async_copy(u_hbm, u_ref, sem.at[1]),
    ]
    for copy in copies:
        copy.start()
    far_kernel(n_rows, True, *x_refs, w0, w1, q1, g1, x_all)
    diff = place_ref[...] - across_ref[...]
    seen = diff >= 0
    diff = jnp.maximum(diff, 0.0)
    for h in range(o_ref.shape[1] // HD):
        cols = slice(h * HD, (h + 1) * HD)
        q = jnp.concatenate([q0[:, cols], q1[:, cols]], 0)
        k = jnp.concatenate([k0[:, cols], k1[:, cols]], 0)
        v = jnp.concatenate([v0[:, cols], v1[:, cols]], 0)
        scores = lax.dot_general(q, k, (((1,), (1,)), ((), ())), preferred_element_type=F32)
        causal = jnp.where(seen, jnp.exp(-rate_ref[h] * diff), 0.0)
        o_ref[:, cols] = jnp.dot(
            (scores * causal).astype(BF16), v, preferred_element_type=F32
        )
    for copy in copies:
        copy.wait()


def middle(rate, down, across, rows, w0, w1, q0, k0, k1, v0, v1, w, u):
    count = sum(r.shape[0] for r in rows)
    depth, width = rows[0].shape[1], w0.shape[1] // 2
    weight = pltpu.VMEM(w.shape, w.dtype)
    return pl.pallas_call(
        functools.partial(middle_kernel, len(rows)),
        in_specs=[SMEM] + [VMEM] * (len(rows) + 9) + [HBM] * 2,
        out_specs=[VMEM] * 5,
        out_shape=[
            pltpu.VMEM((count, width), BF16),
            pltpu.VMEM((count, width), F32),
            pltpu.VMEM((down.shape[0], width), F32),
            weight,
            weight,
        ],
        scratch_shapes=[pltpu.VMEM((count, depth), BF16), pltpu.SemaphoreType.DMA((2,))],
        compiler_params=pltpu.CompilerParams(vmem_limit_bytes=12 * MIB),
        cost_estimate=pl.CostEstimate(
            flops=4 * count * depth * width, bytes_accessed=8 * depth * width, transcendentals=0
        ),
        name="middle",
    )(rate, down, across, *rows, pinned(w0), pinned(w1), q0, k0, k1, v0, v1, in_hbm(w), in_hbm(u))


TO_SUM = (3, 7, 1, 5, 2, 6, 0, 4)


def finish_kernel(rate_ref, place_ref, gain_ref, in_ref, q0, q1, g0, g1, s1, s2, s3, y_ref, z_ref):
    part = in_ref.shape[0] // 8
    for h in range(in_ref.shape[1] // HD):
        cols = slice(h * HD, (h + 1) * HD)
        rate = rate_ref[h]
        span = jnp.exp(jnp.full((HD, HD), -rate * BLOCK, F32))
        state = s1[h].astype(F32) + span * (s2[h].astype(F32) + span * s3[h].astype(F32))
        high = state.astype(BF16)
        low = (state - high.astype(F32)).astype(BF16)
        q = jnp.concatenate([q0[:, cols], q1[:, cols]], 0)
        extra = jnp.dot(q, high, preferred_element_type=F32) + jnp.dot(
            q, low, preferred_element_type=F32
        )
        attn = in_ref[:, cols] + extra * jnp.exp(-rate * (place_ref[...] + 1.0))
        square = jnp.mean(attn * attn, axis=-1, keepdims=True)
        gate = jnp.concatenate([g0[:, cols], g1[:, cols]], 0)
        y = (attn * lax.rsqrt(square + 1e-06) * gain_ref[:, cols] * gate).astype(BF16)
        for slot, to in enumerate(TO_SUM):
            to_ref, at = (y_ref, to) if to < 4 else (z_ref, to - 4)
            to_ref[at * part : (at + 1) * part, cols] = y[slot * part : (slot + 1) * part]


def small(kernel, n_smem, out, name, *args):
    return pl.pallas_call(
        kernel,
        in_specs=[SMEM] * n_smem + [VMEM] * (len(args) - n_smem),
        out_specs=jax.tree.map(lambda _: VMEM, out),
        out_shape=out,
        compiler_params=pltpu.CompilerParams(vmem_limit_bytes=12 * MIB),
        name=name,
    )(*args)


def out_kernel(y_ref, z_ref, w_ref, u_ref, a_ref, b_ref, c_ref, d_ref):
    rows, width = a_ref.shape
    step = 1024
    for at in range(0, width, step):
        cols = slice(at, at + step)
        total = jnp.dot(y_ref[...], w_ref[:, cols], preferred_element_type=F32) + jnp.dot(
            z_ref[...], u_ref[:, cols], preferred_element_type=F32
        )
        for i, ref in enumerate((a_ref, b_ref, c_ref, d_ref)):
            ref[:, cols] = total[i * rows : (i + 1) * rows].astype(ref.dtype)


def out_rows(y, z, w, u):
    rows, depth = y.shape
    width = w.shape[1]
    send = jax.ShapeDtypeStruct((rows // 4, width), BF16)
    keep = jax.ShapeDtypeStruct((rows // 4, width), F32)
    return pl.pallas_call(
        out_kernel,
        in_specs=[VMEM] * 4,
        out_specs=[VMEM] * 4,
        out_shape=[send, keep, send, keep],
        compiler_params=pltpu.CompilerParams(vmem_limit_bytes=16 * MIB),
        cost_estimate=pl.CostEstimate(
            flops=4 * rows * depth * width, bytes_accessed=4 * depth * width, transcendentals=0
        ),
        name="out_rows",
    )(y, z, pinned(w), pinned(u))


def paired_device(tokens, proj_weight, out_weight, head_gain, decay_rate):
    rows = tokens.shape[0]
    heads = decay_rate.shape[0]
    count = lax.axis_size("seq")

    beside = hop(tokens, CORE)
    first = hop(tokens, FIRST)
    second = hop(tokens, SECOND)
    kv0, qg0, down, across = prep(proj_weight, 8 * rows)
    far = hop(first, SECOND)
    first_beside = hop(first, CORE)
    kv1, qg1, k0, v0, q0, g0 = project_near(
        [tokens, beside, first, first_beside], kv0, qg0, proj_weight
    )
    second_beside = hop(second, CORE)
    far_beside = hop(far, CORE)
    w_other = hop(out_weight, CORE)
    late = [second, second_beside, far, far_beside]
    k1, v1 = project_far(late, kv0, kv1, False, "project_far_kv")

    states = small(
        state_kernel,
        1,
        jax.ShapeDtypeStruct((heads, HD, HD), BF16),
        "state",
        decay_rate, down, k0, k1, v0, v1,
    )
    came = [
        lax.ppermute(states, "seq", [(i, i + k) for i in range(count - k)]) for k in range(1, count)
    ]
    q1, g1, inner, w_own, w_other = middle(
        decay_rate, down, across, late, qg0, qg1, q0, k0, k1, v0, v1, out_weight, w_other
    )
    split = jax.ShapeDtypeStruct((4 * rows, heads * HD), BF16)
    y, y_other = small(
        finish_kernel,
        1,
        [split, split],
        "finish",
        decay_rate, down, head_gain[None, :], inner, q0, q1, g0, g1, *came,
    )
    z = hop(y_other, CORE)
    a, b, c, d = out_rows(y, z, w_own, w_other)
    got_a = hop(a, SECOND)
    got_c = hop(c, SECOND)
    got_b = hop((b + got_a.astype(F32)).astype(BF16), FIRST)
    return (d + got_c.astype(F32) + got_b.astype(F32)).astype(BF16)


def solution(mesh):
    paired = mesh.shape["tp"] == 8 and mesh.shape["seq"] == 4
    return jax.shard_map(
        paired_device if paired else general_device,
        mesh=mesh,
        in_specs=(P(("seq", "tp"), None), P(None, None, "tp"), P("tp", None), P("tp"), P("tp")),
        out_specs=P(("seq", "tp"), None),
        check_vma=False,
    )
```

```python
import functools

import jax
import jax.numpy as jnp
from jax import lax
from jax.experimental import pallas as pl
from jax.experimental.pallas import tpu as pltpu
from jax.sharding import PartitionSpec as P

HD = 128
BLOCK = 256
F32, BF16 = jnp.float32, jnp.bfloat16
VMEM = pl.BlockSpec(memory_space=pltpu.VMEM)
SMEM = pl.BlockSpec(memory_space=pltpu.SMEM)
HBM = pl.BlockSpec(memory_space=pl.ANY)
MIB = 1 << 20


def entering(value, axis, combine, identity):
    count, position = (lax.axis_size(axis), lax.axis_index(axis))
    everything = jax.tree.map(
        lambda part, kind: lax.all_gather(part.astype(kind), axis),
        value,
        (jnp.bfloat16, jnp.bfloat16),
    )
    start = jax.tree.map(
        lambda part, zero: jnp.broadcast_to(jnp.asarray(zero, part.dtype), part.shape),
        value,
        identity,
    )

    def turn(k, before):
        reached = k < position
        new = combine(
            before, jax.tree.map(lambda part, own: part[k].astype(own.dtype), everything, value)
        )
        return jax.tree.map(lambda a, b: jnp.where(reached, a, b), new, before)

    return lax.fori_loop(0, count, turn, start)


def attend(q_head, k_head, v_head, rate, start_state):
    count = q_head.shape[0] // BLOCK
    place = jnp.arange(BLOCK).astype(jnp.float32)
    diff = place[:, None] - place[None, :]
    causal = jnp.where(diff >= 0, jnp.exp(-rate * jnp.maximum(diff, 0.0)), 0.0)
    in_decay = jnp.exp(-rate * (place + 1.0))
    out_decay = jnp.exp(-rate * (BLOCK - 1.0 - place))
    block_decay = jnp.exp(-rate * BLOCK)
    q_blocks = q_head.reshape(count, BLOCK, q_head.shape[1])
    k_blocks = k_head.reshape(count, BLOCK, k_head.shape[1])
    v_blocks = v_head.reshape(count, BLOCK, v_head.shape[1])

    def advance(state, block):
        q_blk, k_blk, v_blk = block
        scores = jnp.dot(q_blk, k_blk.T, preferred_element_type=jnp.float32)
        weighted = (scores * causal).astype(jnp.bfloat16)
        inner = jnp.dot(weighted, v_blk, preferred_element_type=jnp.float32)
        carried = (
            jnp.dot(q_blk.astype(jnp.float32), state, precision=lax.Precision.HIGHEST)
            * in_decay[:, None]
        )
        scaled = k_blk.astype(jnp.float32) * out_decay[:, None]
        update = jnp.dot(scaled.T, v_blk.astype(jnp.float32), precision=lax.Precision.HIGHEST)
        return (block_decay * state + update, inner + carried)

    final_state, outputs = lax.scan(advance, start_state, (q_blocks, k_blocks, v_blocks))
    return (outputs.reshape(q_head.shape[0], q_head.shape[1]), final_state)


def general_device(tokens, proj_weight, out_weight, head_gain, decay_rate):
    heads_here = decay_rate.shape[0]
    width = head_gain.shape[0]
    flat = proj_weight.reshape(proj_weight.shape[0], 4 * width)
    mixed = jnp.dot(
        lax.all_gather(tokens, "tp", axis=0, tiled=True), flat, preferred_element_type=jnp.float32
    )
    local_rows = mixed.shape[0]
    q_all = jax.nn.silu(mixed[:, :width]).astype(jnp.bfloat16).reshape(local_rows, heads_here, HD)
    k_all = (
        jax.nn.silu(mixed[:, width : 2 * width])
        .astype(jnp.bfloat16)
        .reshape(local_rows, heads_here, HD)
    )
    v_all = (
        jax.nn.silu(mixed[:, 2 * width : 3 * width])
        .astype(jnp.bfloat16)
        .reshape(local_rows, heads_here, HD)
    )
    gate = mixed[:, 3 * width :].reshape(local_rows, heads_here, HD)
    zero_state = jnp.zeros((HD, HD), jnp.float32)
    outputs, local_states = jax.vmap(attend, in_axes=(1, 1, 1, 0, None), out_axes=(1, 0))(
        q_all, k_all, v_all, decay_rate, zero_state
    )
    zero_states = jnp.zeros((heads_here, HD, HD), jnp.float32)
    span_decay = jnp.exp(-decay_rate * local_rows)

    def combine(earlier, later):
        return (later[1][:, None, None] * earlier[0] + later[0], earlier[1] * later[1])

    incoming, unused = entering(
        (local_states, span_decay), "seq", combine, (zero_states, jnp.ones_like(span_decay))
    )
    place = jnp.arange(local_rows).astype(jnp.float32)
    lift = jnp.exp(-decay_rate[None, :] * (place[:, None] + 1.0))
    extra = jnp.einsum(
        "thd,hde->the", q_all.astype(jnp.float32), incoming, precision=lax.Precision.HIGHEST
    )
    attn = outputs + extra * lift[:, :, None]
    square = jnp.mean(attn * attn, axis=-1, keepdims=True)
    normed = (
        attn
        * lax.rsqrt(square + 1e-06)
        * head_gain.reshape(heads_here, HD)[None]
        * jax.nn.sigmoid(gate)
    )
    joined = normed.astype(jnp.bfloat16).reshape(local_rows, width)
    return lax.psum_scatter(
        jnp.dot(joined, out_weight, preferred_element_type=jnp.float32).astype(jnp.bfloat16),
        "tp",
        scatter_dimension=0,
        tiled=True,
    )


CORE = [(i, i ^ 1) for i in range(8)]
FIRST = [(i, i ^ (4 if i & 1 else 2)) for i in range(8)]
SECOND = [(i, i ^ (2 if i & 1 else 4)) for i in range(8)]


def hop(value, pairs):
    return lax.ppermute(value, "tp", pairs)


STEP = 256
SLOTS = 8


def pinned(value):
    return pltpu.with_memory_space_constraint(value, pltpu.VMEM)


def in_hbm(value):
    return pltpu.with_memory_space_constraint(value, pltpu.HBM)


def chunks(first, count, w_hbm, buf, sem):
    slots, step = buf.shape[:2]

    def copy(i):
        return pltpu.make_async_copy(
            w_hbm.at[pl.ds(first + i * step, step)], buf.at[i % slots], sem.at[i % slots]
        )

    for i in range(min(slots, count)):
        copy(i).start()
    for i in range(count):
        copy(i).wait()
        yield i, buf[i % slots]
        if i + slots < count:
            copy(i + slots).start()


def turn(block, at, kv_ref, qg_ref):
    width = block.shape[2]
    turned = jnp.swapaxes(block, 0, 1)
    kv_ref[at, :width] = turned[1]
    kv_ref[at, width:] = turned[2]
    qg_ref[at, :width] = turned[0]
    qg_ref[at, width:] = turned[3]
    return turned


def slot_places(index, shape, axis):
    row = lax.broadcasted_iota(jnp.int32, shape, axis)
    part = shape[axis] // 8
    core = index & 1
    near = jnp.where(core == 0, 2, 4)
    far = 6 - near
    owners = (
        index,
        index ^ 1,
        index ^ near,
        index ^ far,
        index ^ 1 ^ far,
        index ^ 1 ^ near,
        index ^ 6,
        index ^ 7,
    )
    place = row
    for slot, owner in enumerate(owners):
        place = jnp.where(row // part == slot, row + (owner - slot) * part, place)
    return place.astype(F32)


def tie_kernel(*refs):
    pass


def tie(values, others):
    return pl.pallas_call(
        tie_kernel,
        in_specs=[HBM] * (len(values) + len(others)),
        out_specs=[HBM] * len(values),
        out_shape=[jax.ShapeDtypeStruct(v.shape, v.dtype) for v in values],
        input_output_aliases={i: i for i in range(len(values))},
        compiler_params=pltpu.CompilerParams(vmem_limit_bytes=MIB // 4),
        name="tie",
    )(*values, *others)


def prep_kernel(first, last, started, w_hbm, pass_ref, *refs):
    refs = refs[2 * started :]
    kv_ref, qg_ref, *outs = refs[:-3]
    buf, sem, pass_sem = refs[-3:]
    step = buf.shape[1]
    passing = []
    if len(outs) == 1:
        passing = [pltpu.make_async_copy(pass_ref, outs[0], pass_sem)]
    for copy in passing:
        copy.start()
    for i, block in chunks(first, (last - first) // step, w_hbm, buf, sem):
        if i == 0 and len(outs) == 2:
            index = lax.axis_index("tp")
            for axis, ref in enumerate(outs):
                ref[...] = slot_places(index, ref.shape, axis)
        turn(block, slice(first + i * step, first + (i + 1) * step), kv_ref, qg_ref)
    for copy in passing:
        copy.wait()


def prep(first, last, proj_weight, turned, passed, outs, name):
    depth, kinds, width = proj_weight.shape
    out = pltpu.VMEM((depth, 2 * width), BF16)
    slots = min(SLOTS, (last - first) // STEP)
    return pl.pallas_call(
        functools.partial(prep_kernel, first, last, bool(turned)),
        in_specs=[HBM, HBM] + [VMEM] * len(turned),
        out_specs=[VMEM] * (2 + len(outs)),
        out_shape=[out, out, *outs],
        scratch_shapes=[
            pltpu.VMEM((slots, STEP, kinds, width), BF16),
            pltpu.SemaphoreType.DMA((slots,)),
            pltpu.SemaphoreType.DMA,
        ],
        input_output_aliases={2 + i: i for i in range(len(turned))},
        compiler_params=pltpu.CompilerParams(vmem_limit_bytes=9 * MIB),
        cost_estimate=pl.CostEstimate(
            flops=0, bytes_accessed=4 * (last - first) * kinds * width, transcendentals=0
        ),
        name=name,
    )(in_hbm(proj_weight), passed, *map(pinned, turned))


def gather_rows(x_refs, x_all, at):
    for ref in x_refs:
        x_all[at : at + ref.shape[0], :] = ref[...]
        at += ref.shape[0]


def silu(mixed):
    return (mixed / (1.0 + jnp.exp(-mixed))).astype(BF16)


def near_kernel(n_rows, first, *refs):
    x_refs = refs[:n_rows]
    w_hbm, _, _, kv, qg, x_all, k_ref, v_ref, total, buf, sem = refs[n_rows:]
    step, (count, width) = buf.shape[1], k_ref.shape
    depth = kv.shape[0]
    arriving = chunks(first, (depth - first) // step, w_hbm, buf, sem)
    for c, block in arriving:
        if c == 0:
            gather_rows(x_refs, x_all, 0)
            for i in range(2):
                total[i] = jnp.dot(
                    x_all[:count, :first],
                    kv[:first, i * width : (i + 1) * width],
                    preferred_element_type=F32,
                )
        at = first + c * step
        turned = turn(block, slice(at, at + step), kv, qg)
        for i in range(2):
            total[i] += jnp.dot(
                x_all[:count, at : at + step], turned[1 + i], preferred_element_type=F32
            )
    k_ref[...] = silu(total[0])
    v_ref[...] = silu(total[1])


def project_near(rows, first, proj_weight, kv, qg):
    count = sum(r.shape[0] for r in rows)
    depth, kinds, width = proj_weight.shape
    turned = pltpu.VMEM(kv.shape, BF16)
    half = pltpu.VMEM((count, width), BF16)
    slots = min(SLOTS, (depth - first) // STEP)
    return pl.pallas_call(
        functools.partial(near_kernel, len(rows), first),
        in_specs=[VMEM] * len(rows) + [HBM, VMEM, VMEM],
        out_specs=[VMEM] * 5,
        out_shape=[turned, turned, pltpu.VMEM((2 * count, depth), BF16), half, half],
        scratch_shapes=[
            pltpu.VMEM((2, count, width), F32),
            pltpu.VMEM((slots, STEP, kinds, width), BF16),
            pltpu.SemaphoreType.DMA((slots,)),
        ],
        input_output_aliases={len(rows) + 1: 0, len(rows) + 2: 1},
        compiler_params=pltpu.CompilerParams(vmem_limit_bytes=9 * MIB),
        cost_estimate=pl.CostEstimate(
            flops=2 * count * depth * kinds * width,
            bytes_accessed=4 * depth * kinds * width,
            transcendentals=0,
        ),
        name="project_near",
    )(*rows, in_hbm(proj_weight), pinned(kv), pinned(qg))


def far_kernel(n_rows, rate_ref, place_ref, k0, v0, kv, _, *refs):
    x_refs = refs[:n_rows]
    x_all, k_ref, v_ref, s_ref = refs[n_rows:]
    count, width = k_ref.shape
    gather_rows(x_refs, x_all, count)
    for i, ref in enumerate((k_ref, v_ref)):
        ref[...] = silu(
            jnp.dot(
                x_all[count:],
                kv[:, i * width : (i + 1) * width],
                preferred_element_type=F32,
            )
        )
    for h in range(s_ref.shape[0]):
        cols = slice(h * HD, (h + 1) * HD)
        fade = jnp.exp(-rate_ref[h] * (BLOCK - 1.0 - place_ref[...]))
        k = jnp.concatenate([k0[:, cols], k_ref[:, cols]], 0).astype(F32) * fade
        v = jnp.concatenate([v0[:, cols], v_ref[:, cols]], 0)
        s_ref[h] = lax.dot_general(
            k.astype(BF16), v, (((0,), (0,)), ((), ())), preferred_element_type=F32
        ).astype(BF16)


def project_far(rate, down, k0, v0, kv, x_all, rows):
    count = sum(r.shape[0] for r in rows)
    depth, width = rows[0].shape[1], k0.shape[1]
    half = pltpu.VMEM((count, width), BF16)
    return pl.pallas_call(
        functools.partial(far_kernel, len(rows)),
        in_specs=[SMEM] + [VMEM] * (5 + len(rows)),
        out_specs=[VMEM] * 4,
        out_shape=[
            pltpu.VMEM(x_all.shape, BF16),
            half,
            half,
            jax.ShapeDtypeStruct((rate.shape[0], HD, HD), BF16),
        ],
        input_output_aliases={5: 0},
        compiler_params=pltpu.CompilerParams(vmem_limit_bytes=2 * MIB),
        cost_estimate=pl.CostEstimate(
            flops=4 * count * depth * width, bytes_accessed=4 * depth * width, transcendentals=0
        ),
        name="project_far",
    )(rate, down, k0, v0, pinned(kv), pinned(x_all), *rows)


def block_decay(rate):
    return jnp.exp(jnp.full((HD, HD), -rate * BLOCK, F32))


def carry_kernel(rate_ref, own_ref, came_ref, _, o_ref):
    came = lax.axis_index("seq") > 0
    for h in range(o_ref.shape[0]):
        o_ref[h] = (
            own_ref[h].astype(F32)
            + jnp.where(came, block_decay(rate_ref[h]) * came_ref[h].astype(F32), 0.0)
        ).astype(BF16)


def gates_kernel(x_all, qg, w_hbm, q_ref, g_ref, w_ref, sem):
    copy = pltpu.make_async_copy(w_hbm, w_ref, sem)
    copy.start()
    width = q_ref.shape[1]
    q_ref[...] = silu(jnp.dot(x_all[...], qg[:, :width], preferred_element_type=F32))
    mixed = jnp.dot(x_all[...], qg[:, width:], preferred_element_type=F32)
    g_ref[...] = 1.0 / (1.0 + jnp.exp(-mixed))
    copy.wait()


def gates(x_all, qg, w):
    count, depth = x_all.shape
    width = qg.shape[1] // 2
    return pl.pallas_call(
        gates_kernel,
        in_specs=[VMEM, VMEM, HBM],
        out_specs=[VMEM] * 3,
        out_shape=[
            pltpu.VMEM((count, width), BF16),
            pltpu.VMEM((count, width), F32),
            pltpu.VMEM(w.shape, w.dtype),
        ],
        scratch_shapes=[pltpu.SemaphoreType.DMA],
        compiler_params=pltpu.CompilerParams(vmem_limit_bytes=2 * MIB),
        cost_estimate=pl.CostEstimate(
            flops=4 * count * depth * width, bytes_accessed=8 * depth * width, transcendentals=0
        ),
        name="gates",
    )(pinned(x_all), pinned(qg), in_hbm(w))


def inner_kernel(rate_ref, place_ref, across_ref, q_ref, k0, k1, v0, v1, o_ref):
    diff = place_ref[...] - across_ref[...]
    seen = diff >= 0
    diff = jnp.maximum(diff, 0.0)
    for h in range(o_ref.shape[1] // HD):
        cols = slice(h * HD, (h + 1) * HD)
        k = jnp.concatenate([k0[:, cols], k1[:, cols]], 0)
        v = jnp.concatenate([v0[:, cols], v1[:, cols]], 0)
        scores = lax.dot_general(
            q_ref[:, cols], k, (((1,), (1,)), ((), ())), preferred_element_type=F32
        )
        causal = jnp.where(seen, jnp.exp(-rate_ref[h] * diff), 0.0)
        o_ref[:, cols] = jnp.dot(
            (scores * causal).astype(BF16), v, preferred_element_type=F32
        )


TO_SUM = (3, 7, 1, 2, 5, 6, 0, 4)


def finish_kernel(rate_ref, place_ref, gain_ref, in_ref, q_ref, g_ref, s1, s2, s3, y_ref, z_ref):
    part = in_ref.shape[0] // 8
    block = lax.axis_index("seq")
    for h in range(in_ref.shape[1] // HD):
        cols = slice(h * HD, (h + 1) * HD)
        rate = rate_ref[h]
        fade = block_decay(rate)
        state = jnp.where(block > 0, s1[h].astype(F32), 0.0) + fade * (
            jnp.where(block > 1, s2[h].astype(F32), 0.0)
            + fade * jnp.where(block > 2, s3[h].astype(F32), 0.0)
        )
        high = state.astype(BF16)
        low = (state - high.astype(F32)).astype(BF16)
        q = q_ref[:, cols]
        extra = jnp.dot(q, high, preferred_element_type=F32) + jnp.dot(
            q, low, preferred_element_type=F32
        )
        attn = in_ref[:, cols] + extra * jnp.exp(-rate * (place_ref[...] + 1.0))
        square = jnp.mean(attn * attn, axis=-1, keepdims=True)
        y = (attn * lax.rsqrt(square + 1e-06) * gain_ref[:, cols] * g_ref[:, cols]).astype(BF16)
        for slot, to in enumerate(TO_SUM):
            to_ref, at = (y_ref, to) if to < 4 else (z_ref, to - 4)
            to_ref[at * part : (at + 1) * part, cols] = y[slot * part : (slot + 1) * part]


def small(kernel, n_smem, out, name, *args):
    return pl.pallas_call(
        kernel,
        in_specs=[SMEM] * n_smem + [VMEM] * (len(args) - n_smem),
        out_specs=jax.tree.map(lambda _: VMEM, out),
        out_shape=out,
        compiler_params=pltpu.CompilerParams(vmem_limit_bytes=3 * MIB),
        name=name,
    )(*args)


def out_kernel(y_ref, z_ref, w_ref, u_ref, a_ref, b_ref, c_ref, d_ref):
    rows, width = a_ref.shape
    step = 1024
    for at in range(0, width, step):
        cols = slice(at, at + step)
        total = jnp.dot(y_ref[...], w_ref[:, cols], preferred_element_type=F32) + jnp.dot(
            z_ref[...], u_ref[:, cols], preferred_element_type=F32
        )
        for i, ref in enumerate((a_ref, b_ref, c_ref, d_ref)):
            ref[:, cols] = total[i * rows : (i + 1) * rows].astype(ref.dtype)


def out_rows(y, z, w, u):
    rows, depth = y.shape
    width = w.shape[1]
    send = jax.ShapeDtypeStruct((rows // 4, width), BF16)
    keep = jax.ShapeDtypeStruct((rows // 4, width), F32)
    return pl.pallas_call(
        out_kernel,
        in_specs=[VMEM] * 4,
        out_specs=[VMEM] * 4,
        out_shape=[send, keep, send, keep],
        compiler_params=pltpu.CompilerParams(vmem_limit_bytes=4 * MIB),
        cost_estimate=pl.CostEstimate(
            flops=4 * rows * depth * width, bytes_accessed=4 * depth * width, transcendentals=0
        ),
        name="out_rows",
    )(y, z, pinned(w), pinned(u))


def paired_device(tokens, proj_weight, out_weight, head_gain, decay_rate):
    rows = tokens.shape[0]
    heads = decay_rate.shape[0]

    cuts = [proj_weight.shape[0] * i // 4 for i in range(5)]
    w_other = hop(out_weight, CORE)
    first = hop(tokens, FIRST)
    copied = jax.ShapeDtypeStruct(tokens.shape, tokens.dtype)
    *turned, passed = prep(cuts[0], cuts[1], proj_weight, [], tokens, [copied], "prep_a")
    second = hop(passed, SECOND)
    beside = hop(tokens, CORE)
    places = [pltpu.VMEM((8 * rows, 1), F32), pltpu.VMEM((1, 8 * rows), F32)]
    *turned, down, across = prep(cuts[1], cuts[2], proj_weight, turned, passed, places, "prep_b")
    (first,) = tie([first], [down])
    far = hop(first, SECOND)
    second_beside = hop(first, CORE)
    turned = prep(cuts[2], cuts[3], proj_weight, turned, first, [], "prep_c")
    kv, qg, x_all, k0, v0 = project_near(
        [tokens, beside, first, second], cuts[3], proj_weight, *turned
    )
    first_beside = hop(second, CORE)
    (far,) = tie([far], [k0])
    far_beside = hop(far, CORE)
    x_all, k1, v1, states = project_far(
        decay_rate, down, k0, v0, kv, x_all, [second_beside, first_beside, far, far_beside]
    )

    came = [
        lax.ppermute(states, "seq", [(i, (i + k) % 4) for i in range(4)]) for k in (1, 2, 3)
    ]
    q, g, w_own = gates(x_all, qg, out_weight)
    full = jax.ShapeDtypeStruct((8 * rows, heads * HD), F32)
    inner = small(inner_kernel, 1, full, "inner", decay_rate, down, across, q, k0, k1, v0, v1)
    split = jax.ShapeDtypeStruct((4 * rows, heads * HD), BF16)
    y, y_other = small(
        finish_kernel,
        1,
        [split, split],
        "finish",
        decay_rate, down, head_gain[None, :], inner, q, g, *came,
    )
    z = hop(y_other, CORE)
    a, b, c, d = out_rows(y, z, w_own, w_other)
    got_a = hop(a, SECOND)
    got_c = hop(c, SECOND)
    got_b = hop((b + got_a.astype(F32)).astype(BF16), FIRST)
    return (d + got_c.astype(F32) + got_b.astype(F32)).astype(BF16)


def solution(mesh):
    paired = mesh.shape["tp"] == 8 and mesh.shape["seq"] == 4
    return jax.shard_map(
        paired_device if paired else general_device,
        mesh=mesh,
        in_specs=(P(("seq", "tp"), None), P(None, None, "tp"), P("tp", None), P("tp"), P("tp")),
        out_specs=P(("seq", "tp"), None),
        check_vma=False,
    )
```

```python
import functools

import jax
import jax.numpy as jnp
from jax import lax
from jax.experimental import pallas as pl
from jax.experimental.pallas import tpu as pltpu
from jax.sharding import PartitionSpec as P

HD = 128
BLOCK = 256
F32, BF16 = jnp.float32, jnp.bfloat16
VMEM = pl.BlockSpec(memory_space=pltpu.VMEM)
SMEM = pl.BlockSpec(memory_space=pltpu.SMEM)
HBM = pl.BlockSpec(memory_space=pl.ANY)
MIB = 1 << 20


def entering(value, axis, combine, identity):
    count, position = (lax.axis_size(axis), lax.axis_index(axis))
    everything = jax.tree.map(
        lambda part, kind: lax.all_gather(part.astype(kind), axis),
        value,
        (jnp.bfloat16, jnp.bfloat16),
    )
    start = jax.tree.map(
        lambda part, zero: jnp.broadcast_to(jnp.asarray(zero, part.dtype), part.shape),
        value,
        identity,
    )

    def turn(k, before):
        reached = k < position
        new = combine(
            before, jax.tree.map(lambda part, own: part[k].astype(own.dtype), everything, value)
        )
        return jax.tree.map(lambda a, b: jnp.where(reached, a, b), new, before)

    return lax.fori_loop(0, count, turn, start)


def attend(q_head, k_head, v_head, rate, start_state):
    count = q_head.shape[0] // BLOCK
    place = jnp.arange(BLOCK).astype(jnp.float32)
    diff = place[:, None] - place[None, :]
    causal = jnp.where(diff >= 0, jnp.exp(-rate * jnp.maximum(diff, 0.0)), 0.0)
    in_decay = jnp.exp(-rate * (place + 1.0))
    out_decay = jnp.exp(-rate * (BLOCK - 1.0 - place))
    block_decay = jnp.exp(-rate * BLOCK)
    q_blocks = q_head.reshape(count, BLOCK, q_head.shape[1])
    k_blocks = k_head.reshape(count, BLOCK, k_head.shape[1])
    v_blocks = v_head.reshape(count, BLOCK, v_head.shape[1])

    def advance(state, block):
        q_blk, k_blk, v_blk = block
        scores = jnp.dot(q_blk, k_blk.T, preferred_element_type=jnp.float32)
        weighted = (scores * causal).astype(jnp.bfloat16)
        inner = jnp.dot(weighted, v_blk, preferred_element_type=jnp.float32)
        carried = (
            jnp.dot(q_blk.astype(jnp.float32), state, precision=lax.Precision.HIGHEST)
            * in_decay[:, None]
        )
        scaled = k_blk.astype(jnp.float32) * out_decay[:, None]
        update = jnp.dot(scaled.T, v_blk.astype(jnp.float32), precision=lax.Precision.HIGHEST)
        return (block_decay * state + update, inner + carried)

    final_state, outputs = lax.scan(advance, start_state, (q_blocks, k_blocks, v_blocks))
    return (outputs.reshape(q_head.shape[0], q_head.shape[1]), final_state)


def general_device(tokens, proj_weight, out_weight, head_gain, decay_rate):
    heads_here = decay_rate.shape[0]
    width = head_gain.shape[0]
    flat = proj_weight.reshape(proj_weight.shape[0], 4 * width)
    mixed = jnp.dot(
        lax.all_gather(tokens, "tp", axis=0, tiled=True), flat, preferred_element_type=jnp.float32
    )
    local_rows = mixed.shape[0]
    q_all = jax.nn.silu(mixed[:, :width]).astype(jnp.bfloat16).reshape(local_rows, heads_here, HD)
    k_all = (
        jax.nn.silu(mixed[:, width : 2 * width])
        .astype(jnp.bfloat16)
        .reshape(local_rows, heads_here, HD)
    )
    v_all = (
        jax.nn.silu(mixed[:, 2 * width : 3 * width])
        .astype(jnp.bfloat16)
        .reshape(local_rows, heads_here, HD)
    )
    gate = mixed[:, 3 * width :].reshape(local_rows, heads_here, HD)
    zero_state = jnp.zeros((HD, HD), jnp.float32)
    outputs, local_states = jax.vmap(attend, in_axes=(1, 1, 1, 0, None), out_axes=(1, 0))(
        q_all, k_all, v_all, decay_rate, zero_state
    )
    zero_states = jnp.zeros((heads_here, HD, HD), jnp.float32)
    span_decay = jnp.exp(-decay_rate * local_rows)

    def combine(earlier, later):
        return (later[1][:, None, None] * earlier[0] + later[0], earlier[1] * later[1])

    incoming, unused = entering(
        (local_states, span_decay), "seq", combine, (zero_states, jnp.ones_like(span_decay))
    )
    place = jnp.arange(local_rows).astype(jnp.float32)
    lift = jnp.exp(-decay_rate[None, :] * (place[:, None] + 1.0))
    extra = jnp.einsum(
        "thd,hde->the", q_all.astype(jnp.float32), incoming, precision=lax.Precision.HIGHEST
    )
    attn = outputs + extra * lift[:, :, None]
    square = jnp.mean(attn * attn, axis=-1, keepdims=True)
    normed = (
        attn
        * lax.rsqrt(square + 1e-06)
        * head_gain.reshape(heads_here, HD)[None]
        * jax.nn.sigmoid(gate)
    )
    joined = normed.astype(jnp.bfloat16).reshape(local_rows, width)
    return lax.psum_scatter(
        jnp.dot(joined, out_weight, preferred_element_type=jnp.float32).astype(jnp.bfloat16),
        "tp",
        scatter_dimension=0,
        tiled=True,
    )


CORE = [(i, i ^ 1) for i in range(8)]
FIRST = [(i, i ^ (4 if i & 1 else 2)) for i in range(8)]
SECOND = [(i, i ^ (2 if i & 1 else 4)) for i in range(8)]


def hop(value, pairs):
    return lax.ppermute(value, "tp", pairs)


STEP = 256
SLOTS = 8


def pinned(value):
    return pltpu.with_memory_space_constraint(value, pltpu.VMEM)


def in_hbm(value):
    return pltpu.with_memory_space_constraint(value, pltpu.HBM)


def chunks(first, count, w_hbm, buf, sem):
    slots, step = buf.shape[:2]

    def copy(i):
        return pltpu.make_async_copy(
            w_hbm.at[pl.ds(first + i * step, step)], buf.at[i % slots], sem.at[i % slots]
        )

    def arriving():
        for i in range(count):
            copy(i).wait()
            yield i, buf[i % slots]
            if i + slots < count:
                copy(i + slots).start()

    for i in range(min(slots, count)):
        copy(i).start()
    return arriving()


def turn(block, at, kv_ref, qg_ref):
    width = block.shape[2]
    turned = jnp.swapaxes(block, 0, 1)
    kv_ref[at, :width] = turned[1]
    kv_ref[at, width:] = turned[2]
    qg_ref[at, :width] = turned[0]
    qg_ref[at, width:] = turned[3]
    return turned


def slot_places(index, shape, axis):
    row = lax.broadcasted_iota(jnp.int32, shape, axis)
    part = shape[axis] // 8
    core = index & 1
    near = jnp.where(core == 0, 2, 4)
    far = 6 - near
    owners = (
        index,
        index ^ 1,
        index ^ near,
        index ^ far,
        index ^ 1 ^ far,
        index ^ 1 ^ near,
        index ^ 6,
        index ^ 7,
    )
    place = row
    for slot, owner in enumerate(owners):
        place = jnp.where(row // part == slot, row + (owner - slot) * part, place)
    return place.astype(F32)


def tie_kernel(*refs):
    pass


def tie(values, others):
    return pl.pallas_call(
        tie_kernel,
        in_specs=[HBM] * (len(values) + len(others)),
        out_specs=[HBM] * len(values),
        out_shape=[jax.ShapeDtypeStruct(v.shape, v.dtype) for v in values],
        input_output_aliases={i: i for i in range(len(values))},
        compiler_params=pltpu.CompilerParams(vmem_limit_bytes=MIB // 4),
        name="tie",
    )(*values, *others)


def prep_kernel(first, last, started, w_hbm, pass_ref, *refs):
    refs = refs[2 * started :]
    kv_ref, qg_ref, *outs = refs[:-3]
    buf, sem, pass_sem = refs[-3:]
    step = buf.shape[1]
    passing = []
    if len(outs) == 1:
        passing = [pltpu.make_async_copy(pass_ref, outs[0], pass_sem)]
    for copy in passing:
        copy.start()
    arriving = chunks(first, (last - first) // step, w_hbm, buf, sem)
    if len(outs) == 2:
        index = lax.axis_index("tp")
        for axis, ref in enumerate(outs):
            ref[...] = slot_places(index, ref.shape, axis)
    for i, block in arriving:
        turn(block, slice(first + i * step, first + (i + 1) * step), kv_ref, qg_ref)
    for copy in passing:
        copy.wait()


def prep(first, last, proj_weight, turned, passed, outs, name):
    depth, kinds, width = proj_weight.shape
    out = pltpu.VMEM((depth, 2 * width), BF16)
    slots = min(SLOTS, (last - first) // STEP)
    return pl.pallas_call(
        functools.partial(prep_kernel, first, last, bool(turned)),
        in_specs=[HBM, HBM] + [VMEM] * len(turned),
        out_specs=[VMEM] * (2 + len(outs)),
        out_shape=[out, out, *outs],
        scratch_shapes=[
            pltpu.VMEM((slots, STEP, kinds, width), BF16),
            pltpu.SemaphoreType.DMA((slots,)),
            pltpu.SemaphoreType.DMA,
        ],
        input_output_aliases={2 + i: i for i in range(len(turned))},
        compiler_params=pltpu.CompilerParams(vmem_limit_bytes=11 * MIB),
        cost_estimate=pl.CostEstimate(
            flops=0, bytes_accessed=4 * (last - first) * kinds * width, transcendentals=0
        ),
        name=name,
    )(in_hbm(proj_weight), in_hbm(passed), *map(pinned, turned))


def gather_rows(x_refs, x_all, at):
    for ref in x_refs:
        x_all[at : at + ref.shape[0], :] = ref[...]
        at += ref.shape[0]


def silu(mixed):
    return (mixed / (1.0 + jnp.exp(-mixed))).astype(BF16)


def near_kernel(n_rows, first, *refs):
    x_refs = refs[:n_rows]
    w_hbm, _, _, kv, qg, x_all, k_ref, v_ref, total, buf, sem = refs[n_rows:]
    step, (count, width) = buf.shape[1], k_ref.shape
    depth = kv.shape[0]
    arriving = chunks(first, (depth - first) // step, w_hbm, buf, sem)
    gather_rows(x_refs, x_all, 0)
    for i in range(2):
        total[i] = jnp.dot(
            x_all[:count, :first],
            kv[:first, i * width : (i + 1) * width],
            preferred_element_type=F32,
        )
    for c, block in arriving:
        at = first + c * step
        turned = turn(block, slice(at, at + step), kv, qg)
        for i in range(2):
            total[i] += jnp.dot(
                x_all[:count, at : at + step], turned[1 + i], preferred_element_type=F32
            )
    k_ref[...] = silu(total[0])
    v_ref[...] = silu(total[1])


def project_near(rows, first, proj_weight, kv, qg):
    count = sum(r.shape[0] for r in rows)
    depth, kinds, width = proj_weight.shape
    turned = pltpu.VMEM(kv.shape, BF16)
    half = pltpu.VMEM((count, width), BF16)
    slots = min(SLOTS, (depth - first) // STEP)
    return pl.pallas_call(
        functools.partial(near_kernel, len(rows), first),
        in_specs=[VMEM] * len(rows) + [HBM, VMEM, VMEM],
        out_specs=[VMEM] * 5,
        out_shape=[turned, turned, pltpu.VMEM((2 * count, depth), BF16), half, half],
        scratch_shapes=[
            pltpu.VMEM((2, count, width), F32),
            pltpu.VMEM((slots, STEP, kinds, width), BF16),
            pltpu.SemaphoreType.DMA((slots,)),
        ],
        input_output_aliases={len(rows) + 1: 0, len(rows) + 2: 1},
        compiler_params=pltpu.CompilerParams(vmem_limit_bytes=11 * MIB),
        cost_estimate=pl.CostEstimate(
            flops=2 * count * depth * kinds * width,
            bytes_accessed=4 * depth * kinds * width,
            transcendentals=0,
        ),
        name="project_near",
    )(*rows, in_hbm(proj_weight), pinned(kv), pinned(qg))


def far_kernel(n_rows, rate_ref, place_ref, k0, v0, kv, _, *refs):
    x_refs = refs[:n_rows]
    x_all, k_ref, v_ref, s_ref = refs[n_rows:]
    count, width = k_ref.shape
    gather_rows(x_refs, x_all, count)
    for i, ref in enumerate((k_ref, v_ref)):
        ref[...] = silu(
            jnp.dot(
                x_all[count:],
                kv[:, i * width : (i + 1) * width],
                preferred_element_type=F32,
            )
        )
    for h in range(s_ref.shape[0]):
        cols = slice(h * HD, (h + 1) * HD)
        fade = jnp.exp(-rate_ref[h] * (BLOCK - 1.0 - place_ref[...]))
        k = jnp.concatenate([k0[:, cols], k_ref[:, cols]], 0).astype(F32) * fade
        v = jnp.concatenate([v0[:, cols], v_ref[:, cols]], 0)
        s_ref[h] = lax.dot_general(
            k.astype(BF16), v, (((0,), (0,)), ((), ())), preferred_element_type=F32
        ).astype(BF16)


def project_far(rate, down, k0, v0, kv, x_all, rows):
    count = sum(r.shape[0] for r in rows)
    depth, width = rows[0].shape[1], k0.shape[1]
    half = pltpu.VMEM((count, width), BF16)
    return pl.pallas_call(
        functools.partial(far_kernel, len(rows)),
        in_specs=[SMEM] + [VMEM] * (5 + len(rows)),
        out_specs=[VMEM] * 4,
        out_shape=[
            pltpu.VMEM(x_all.shape, BF16),
            half,
            half,
            jax.ShapeDtypeStruct((rate.shape[0], HD, HD), BF16),
        ],
        input_output_aliases={5: 0},
        compiler_params=pltpu.CompilerParams(vmem_limit_bytes=2 * MIB),
        cost_estimate=pl.CostEstimate(
            flops=4 * count * depth * width, bytes_accessed=4 * depth * width, transcendentals=0
        ),
        name="project_far",
    )(rate, down, k0, v0, pinned(kv), pinned(x_all), *rows)


def block_decay(rate):
    return jnp.exp(jnp.full((HD, HD), -rate * BLOCK, F32))


def carry_kernel(rate_ref, own_ref, came_ref, _, o_ref):
    came = lax.axis_index("seq") > 0
    for h in range(o_ref.shape[0]):
        o_ref[h] = (
            own_ref[h].astype(F32)
            + jnp.where(came, block_decay(rate_ref[h]) * came_ref[h].astype(F32), 0.0)
        ).astype(BF16)


def gates_kernel(x_all, qg, w_hbm, q_ref, g_ref, w_ref, sem):
    copy = pltpu.make_async_copy(w_hbm, w_ref, sem)
    copy.start()
    width = q_ref.shape[1]
    q_ref[...] = silu(jnp.dot(x_all[...], qg[:, :width], preferred_element_type=F32))
    mixed = jnp.dot(x_all[...], qg[:, width:], preferred_element_type=F32)
    g_ref[...] = 1.0 / (1.0 + jnp.exp(-mixed))
    copy.wait()


def gates(x_all, qg, w):
    count, depth = x_all.shape
    width = qg.shape[1] // 2
    return pl.pallas_call(
        gates_kernel,
        in_specs=[VMEM, VMEM, HBM],
        out_specs=[VMEM] * 3,
        out_shape=[
            pltpu.VMEM((count, width), BF16),
            pltpu.VMEM((count, width), F32),
            pltpu.VMEM(w.shape, w.dtype),
        ],
        scratch_shapes=[pltpu.SemaphoreType.DMA],
        compiler_params=pltpu.CompilerParams(vmem_limit_bytes=2 * MIB),
        cost_estimate=pl.CostEstimate(
            flops=4 * count * depth * width, bytes_accessed=8 * depth * width, transcendentals=0
        ),
        name="gates",
    )(pinned(x_all), pinned(qg), in_hbm(w))


def inner_kernel(rate_ref, place_ref, across_ref, q_ref, k0, k1, v0, v1, o_ref):
    diff = place_ref[...] - across_ref[...]
    seen = diff >= 0
    diff = jnp.maximum(diff, 0.0)
    for h in range(o_ref.shape[1] // HD):
        cols = slice(h * HD, (h + 1) * HD)
        k = jnp.concatenate([k0[:, cols], k1[:, cols]], 0)
        v = jnp.concatenate([v0[:, cols], v1[:, cols]], 0)
        scores = lax.dot_general(
            q_ref[:, cols], k, (((1,), (1,)), ((), ())), preferred_element_type=F32
        )
        causal = jnp.where(seen, jnp.exp(-rate_ref[h] * diff), 0.0)
        o_ref[:, cols] = jnp.dot(
            (scores * causal).astype(BF16), v, preferred_element_type=F32
        )


TO_SUM = (3, 7, 1, 2, 5, 6, 0, 4)


def finish_kernel(rate_ref, place_ref, gain_ref, in_ref, q_ref, g_ref, s1, s2, s3, y_ref, z_ref):
    part = in_ref.shape[0] // 8
    block = lax.axis_index("seq")
    for h in range(in_ref.shape[1] // HD):
        cols = slice(h * HD, (h + 1) * HD)
        rate = rate_ref[h]
        fade = block_decay(rate)
        state = jnp.where(block > 0, s1[h].astype(F32), 0.0) + fade * (
            jnp.where(block > 1, s2[h].astype(F32), 0.0)
            + fade * jnp.where(block > 2, s3[h].astype(F32), 0.0)
        )
        high = state.astype(BF16)
        low = (state - high.astype(F32)).astype(BF16)
        q = q_ref[:, cols]
        extra = jnp.dot(q, high, preferred_element_type=F32) + jnp.dot(
            q, low, preferred_element_type=F32
        )
        attn = in_ref[:, cols] + extra * jnp.exp(-rate * (place_ref[...] + 1.0))
        square = jnp.mean(attn * attn, axis=-1, keepdims=True)
        y = (attn * lax.rsqrt(square + 1e-06) * gain_ref[:, cols] * g_ref[:, cols]).astype(BF16)
        for slot, to in enumerate(TO_SUM):
            to_ref, at = (y_ref, to) if to < 4 else (z_ref, to - 4)
            to_ref[at * part : (at + 1) * part, cols] = y[slot * part : (slot + 1) * part]


def small(kernel, n_smem, out, name, *args):
    return pl.pallas_call(
        kernel,
        in_specs=[SMEM] * n_smem + [VMEM] * (len(args) - n_smem),
        out_specs=jax.tree.map(lambda _: VMEM, out),
        out_shape=out,
        compiler_params=pltpu.CompilerParams(vmem_limit_bytes=3 * MIB),
        name=name,
    )(*args)


def out_own_kernel(y_ref, w_ref, o_ref):
    step = 1024
    for at in range(0, o_ref.shape[1], step):
        cols = slice(at, at + step)
        o_ref[:, cols] = jnp.dot(y_ref[...], w_ref[:, cols], preferred_element_type=F32)


def out_own(y, w):
    rows, depth = y.shape
    width = w.shape[1]
    return pl.pallas_call(
        out_own_kernel,
        in_specs=[VMEM] * 2,
        out_specs=VMEM,
        out_shape=pltpu.VMEM((rows, width), F32),
        compiler_params=pltpu.CompilerParams(vmem_limit_bytes=4 * MIB),
        cost_estimate=pl.CostEstimate(
            flops=2 * rows * depth * width, bytes_accessed=2 * depth * width, transcendentals=0
        ),
        name="out_own",
    )(y, pinned(w))


def out_kernel(own_ref, z_ref, u_ref, a_ref, b_ref, c_ref, d_ref):
    rows, width = a_ref.shape
    step = 1024
    for at in range(0, width, step):
        cols = slice(at, at + step)
        total = own_ref[:, cols] + jnp.dot(
            z_ref[...], u_ref[:, cols], preferred_element_type=F32
        )
        for i, ref in enumerate((a_ref, b_ref, c_ref, d_ref)):
            ref[:, cols] = total[i * rows : (i + 1) * rows].astype(ref.dtype)


def out_rows(own, z, u):
    rows, width = own.shape
    send = jax.ShapeDtypeStruct((rows // 4, width), BF16)
    keep = jax.ShapeDtypeStruct((rows // 4, width), F32)
    return pl.pallas_call(
        out_kernel,
        in_specs=[VMEM] * 3,
        out_specs=[VMEM] * 4,
        out_shape=[send, keep, send, keep],
        compiler_params=pltpu.CompilerParams(vmem_limit_bytes=4 * MIB),
        cost_estimate=pl.CostEstimate(
            flops=2 * rows * z.shape[1] * width,
            bytes_accessed=2 * z.shape[1] * width,
            transcendentals=0,
        ),
        name="out_rows",
    )(pinned(own), z, pinned(u))


def paired_device(tokens, proj_weight, out_weight, head_gain, decay_rate):
    rows = tokens.shape[0]
    heads = decay_rate.shape[0]

    cuts = [proj_weight.shape[0] * i // 4 for i in range(5)]
    w_other = hop(out_weight, CORE)
    first = hop(tokens, FIRST)
    copied = jax.ShapeDtypeStruct(tokens.shape, tokens.dtype)
    *turned, passed = prep(cuts[0], cuts[1], proj_weight, [], tokens, [copied], "prep_a")
    second = hop(passed, SECOND)
    beside = hop(tokens, CORE)
    places = [pltpu.VMEM((8 * rows, 1), F32), pltpu.VMEM((1, 8 * rows), F32)]
    *turned, down, across = prep(cuts[1], cuts[2], proj_weight, turned, tokens, places, "prep_b")
    (first,) = tie([first], [down])
    far = hop(first, SECOND)
    second_beside = hop(first, CORE)
    turned = prep(cuts[2], cuts[3], proj_weight, turned, tokens, [], "prep_c")
    kv, qg, x_all, k0, v0 = project_near(
        [tokens, beside, first, second], cuts[3], proj_weight, *turned
    )
    first_beside = hop(second, CORE)
    (far,) = tie([far], [k0])
    far_beside = hop(far, CORE)
    x_all, k1, v1, states = project_far(
        decay_rate, down, k0, v0, kv, x_all, [second_beside, first_beside, far, far_beside]
    )

    came = [
        lax.ppermute(states, "seq", [(i, (i + k) % 4) for i in range(4)]) for k in (1, 2, 3)
    ]
    q, g, w_own = gates(x_all, qg, out_weight)
    full = jax.ShapeDtypeStruct((8 * rows, heads * HD), F32)
    inner = small(inner_kernel, 1, full, "inner", decay_rate, down, across, q, k0, k1, v0, v1)
    split = jax.ShapeDtypeStruct((4 * rows, heads * HD), BF16)
    y, y_other = small(
        finish_kernel,
        1,
        [split, split],
        "finish",
        decay_rate, down, head_gain[None, :], inner, q, g, *came,
    )
    z = hop(y_other, CORE)
    a, b, c, d = out_rows(out_own(y, w_own), z, w_other)
    got_a = hop(a, SECOND)
    got_c = hop(c, SECOND)
    got_b = hop((b + got_a.astype(F32)).astype(BF16), FIRST)
    summed = lax.optimization_barrier(d + got_c.astype(F32))
    return (summed + got_b.astype(F32)).astype(BF16)


def solution(mesh):
    paired = mesh.shape["tp"] == 8 and mesh.shape["seq"] == 4
    return jax.shard_map(
        paired_device if paired else general_device,
        mesh=mesh,
        in_specs=(P(("seq", "tp"), None), P(None, None, "tp"), P("tp", None), P("tp"), P("tp")),
        out_specs=P(("seq", "tp"), None),
        check_vma=False,
    )
```

```python
import functools

import jax
import jax.numpy as jnp
from jax import lax
from jax.experimental import pallas as pl
from jax.experimental.pallas import tpu as pltpu
from jax.sharding import PartitionSpec as P

HD = 128
BLOCK = 256
F32, BF16 = jnp.float32, jnp.bfloat16
VMEM = pl.BlockSpec(memory_space=pltpu.VMEM)
SMEM = pl.BlockSpec(memory_space=pltpu.SMEM)
HBM = pl.BlockSpec(memory_space=pl.ANY)
MIB = 1 << 20


def entering(value, axis, combine, identity):
    count, position = (lax.axis_size(axis), lax.axis_index(axis))
    everything = jax.tree.map(
        lambda part, kind: lax.all_gather(part.astype(kind), axis),
        value,
        (jnp.bfloat16, jnp.bfloat16),
    )
    start = jax.tree.map(
        lambda part, zero: jnp.broadcast_to(jnp.asarray(zero, part.dtype), part.shape),
        value,
        identity,
    )

    def turn(k, before):
        reached = k < position
        new = combine(
            before, jax.tree.map(lambda part, own: part[k].astype(own.dtype), everything, value)
        )
        return jax.tree.map(lambda a, b: jnp.where(reached, a, b), new, before)

    return lax.fori_loop(0, count, turn, start)


def attend(q_head, k_head, v_head, rate, start_state):
    count = q_head.shape[0] // BLOCK
    place = jnp.arange(BLOCK).astype(jnp.float32)
    diff = place[:, None] - place[None, :]
    causal = jnp.where(diff >= 0, jnp.exp(-rate * jnp.maximum(diff, 0.0)), 0.0)
    in_decay = jnp.exp(-rate * (place + 1.0))
    out_decay = jnp.exp(-rate * (BLOCK - 1.0 - place))
    block_decay = jnp.exp(-rate * BLOCK)
    q_blocks = q_head.reshape(count, BLOCK, q_head.shape[1])
    k_blocks = k_head.reshape(count, BLOCK, k_head.shape[1])
    v_blocks = v_head.reshape(count, BLOCK, v_head.shape[1])

    def advance(state, block):
        q_blk, k_blk, v_blk = block
        scores = jnp.dot(q_blk, k_blk.T, preferred_element_type=jnp.float32)
        weighted = (scores * causal).astype(jnp.bfloat16)
        inner = jnp.dot(weighted, v_blk, preferred_element_type=jnp.float32)
        carried = (
            jnp.dot(q_blk.astype(jnp.float32), state, precision=lax.Precision.HIGHEST)
            * in_decay[:, None]
        )
        scaled = k_blk.astype(jnp.float32) * out_decay[:, None]
        update = jnp.dot(scaled.T, v_blk.astype(jnp.float32), precision=lax.Precision.HIGHEST)
        return (block_decay * state + update, inner + carried)

    final_state, outputs = lax.scan(advance, start_state, (q_blocks, k_blocks, v_blocks))
    return (outputs.reshape(q_head.shape[0], q_head.shape[1]), final_state)


def general_device(tokens, proj_weight, out_weight, head_gain, decay_rate):
    heads_here = decay_rate.shape[0]
    width = head_gain.shape[0]
    flat = proj_weight.reshape(proj_weight.shape[0], 4 * width)
    mixed = jnp.dot(
        lax.all_gather(tokens, "tp", axis=0, tiled=True), flat, preferred_element_type=jnp.float32
    )
    local_rows = mixed.shape[0]
    q_all = jax.nn.silu(mixed[:, :width]).astype(jnp.bfloat16).reshape(local_rows, heads_here, HD)
    k_all = (
        jax.nn.silu(mixed[:, width : 2 * width])
        .astype(jnp.bfloat16)
        .reshape(local_rows, heads_here, HD)
    )
    v_all = (
        jax.nn.silu(mixed[:, 2 * width : 3 * width])
        .astype(jnp.bfloat16)
        .reshape(local_rows, heads_here, HD)
    )
    gate = mixed[:, 3 * width :].reshape(local_rows, heads_here, HD)
    zero_state = jnp.zeros((HD, HD), jnp.float32)
    outputs, local_states = jax.vmap(attend, in_axes=(1, 1, 1, 0, None), out_axes=(1, 0))(
        q_all, k_all, v_all, decay_rate, zero_state
    )
    zero_states = jnp.zeros((heads_here, HD, HD), jnp.float32)
    span_decay = jnp.exp(-decay_rate * local_rows)

    def combine(earlier, later):
        return (later[1][:, None, None] * earlier[0] + later[0], earlier[1] * later[1])

    incoming, unused = entering(
        (local_states, span_decay), "seq", combine, (zero_states, jnp.ones_like(span_decay))
    )
    place = jnp.arange(local_rows).astype(jnp.float32)
    lift = jnp.exp(-decay_rate[None, :] * (place[:, None] + 1.0))
    extra = jnp.einsum(
        "thd,hde->the", q_all.astype(jnp.float32), incoming, precision=lax.Precision.HIGHEST
    )
    attn = outputs + extra * lift[:, :, None]
    square = jnp.mean(attn * attn, axis=-1, keepdims=True)
    normed = (
        attn
        * lax.rsqrt(square + 1e-06)
        * head_gain.reshape(heads_here, HD)[None]
        * jax.nn.sigmoid(gate)
    )
    joined = normed.astype(jnp.bfloat16).reshape(local_rows, width)
    return lax.psum_scatter(
        jnp.dot(joined, out_weight, preferred_element_type=jnp.float32).astype(jnp.bfloat16),
        "tp",
        scatter_dimension=0,
        tiled=True,
    )


CORE = [(i, i ^ 1) for i in range(8)]
FIRST = [(i, i ^ (4 if i & 1 else 2)) for i in range(8)]
SECOND = [(i, i ^ (2 if i & 1 else 4)) for i in range(8)]


def hop(value, pairs):
    return lax.ppermute(value, "tp", pairs)


STEP = 256
SLOTS = 8


def pinned(value):
    return pltpu.with_memory_space_constraint(value, pltpu.VMEM)


def in_hbm(value):
    return pltpu.with_memory_space_constraint(value, pltpu.HBM)


def chunks(first, count, w_hbm, buf, sem):
    slots, step = buf.shape[:2]

    def copy(i):
        return pltpu.make_async_copy(
            w_hbm.at[pl.ds(first + i * step, step)], buf.at[i % slots], sem.at[i % slots]
        )

    def arriving():
        for i in range(count):
            copy(i).wait()
            yield i, buf[i % slots]
            if i + slots < count:
                copy(i + slots).start()

    for i in range(min(slots, count)):
        copy(i).start()
    return arriving()


def turn(block, at, kv_ref, qg_ref):
    width = block.shape[2]
    turned = jnp.swapaxes(block, 0, 1)
    kv_ref[at, :width] = turned[1]
    kv_ref[at, width:] = turned[2]
    qg_ref[at, :width] = turned[0]
    qg_ref[at, width:] = turned[3]
    return turned


def slot_places(index, shape, axis):
    row = lax.broadcasted_iota(jnp.int32, shape, axis)
    part = shape[axis] // 8
    core = index & 1
    near = jnp.where(core == 0, 2, 4)
    far = 6 - near
    owners = (
        index,
        index ^ 1,
        index ^ near,
        index ^ far,
        index ^ 1 ^ far,
        index ^ 1 ^ near,
        index ^ 6,
        index ^ 7,
    )
    place = row
    for slot, owner in enumerate(owners):
        place = jnp.where(row // part == slot, row + (owner - slot) * part, place)
    return place.astype(F32)


def tie_kernel(*refs):
    pass


def tie(values, others):
    return pl.pallas_call(
        tie_kernel,
        in_specs=[HBM] * (len(values) + len(others)),
        out_specs=[HBM] * len(values),
        out_shape=[jax.ShapeDtypeStruct(v.shape, v.dtype) for v in values],
        input_output_aliases={i: i for i in range(len(values))},
        compiler_params=pltpu.CompilerParams(vmem_limit_bytes=MIB // 4),
        name="tie",
    )(*values, *others)


def prep_kernel(first, last, started, w_hbm, pass_ref, *refs):
    refs = refs[2 * started :]
    kv_ref, qg_ref, *outs = refs[:-3]
    buf, sem, pass_sem = refs[-3:]
    step = buf.shape[1]
    passing = []
    if outs:
        passing = [pltpu.make_async_copy(pass_ref, outs[0], pass_sem)]
    for copy in passing:
        copy.start()
    arriving = chunks(first, (last - first) // step, w_hbm, buf, sem)
    if outs:
        index = lax.axis_index("tp")
        for axis, ref in enumerate(outs[1:]):
            ref[...] = slot_places(index, ref.shape, axis)
    for i, block in arriving:
        turn(block, slice(first + i * step, first + (i + 1) * step), kv_ref, qg_ref)
    for copy in passing:
        copy.wait()


def prep(first, last, proj_weight, turned, passed, outs, name):
    depth, kinds, width = proj_weight.shape
    out = pltpu.VMEM((depth, 2 * width), BF16)
    slots = min(SLOTS, (last - first) // STEP)
    return pl.pallas_call(
        functools.partial(prep_kernel, first, last, bool(turned)),
        in_specs=[HBM, HBM] + [VMEM] * len(turned),
        out_specs=[VMEM] * (2 + len(outs)),
        out_shape=[out, out, *outs],
        scratch_shapes=[
            pltpu.VMEM((slots, STEP, kinds, width), BF16),
            pltpu.SemaphoreType.DMA((slots,)),
            pltpu.SemaphoreType.DMA,
        ],
        input_output_aliases={2 + i: i for i in range(len(turned))},
        compiler_params=pltpu.CompilerParams(vmem_limit_bytes=11 * MIB),
        cost_estimate=pl.CostEstimate(
            flops=0, bytes_accessed=4 * (last - first) * kinds * width, transcendentals=0
        ),
        name=name,
    )(in_hbm(proj_weight), in_hbm(passed), *map(pinned, turned))


def gather_rows(x_refs, x_all, at):
    for ref in x_refs:
        x_all[at : at + ref.shape[0], :] = ref[...]
        at += ref.shape[0]


def silu(mixed):
    return (mixed / (1.0 + jnp.exp(-mixed))).astype(BF16)


def near_kernel(n_rows, first, *refs):
    x_refs = refs[:n_rows]
    w_hbm, _, _, kv, qg, x_all, k_ref, v_ref, total, buf, sem = refs[n_rows:]
    step, (count, width) = buf.shape[1], k_ref.shape
    depth = kv.shape[0]
    arriving = chunks(first, (depth - first) // step, w_hbm, buf, sem)
    gather_rows(x_refs, x_all, 0)
    for i in range(2):
        total[i] = jnp.dot(
            x_all[:count, :first],
            kv[:first, i * width : (i + 1) * width],
            preferred_element_type=F32,
        )
    for c, block in arriving:
        at = first + c * step
        turned = turn(block, slice(at, at + step), kv, qg)
        for i in range(2):
            total[i] += jnp.dot(
                x_all[:count, at : at + step], turned[1 + i], preferred_element_type=F32
            )
    k_ref[...] = silu(total[0])
    v_ref[...] = silu(total[1])


def project_near(rows, first, proj_weight, kv, qg):
    count = sum(r.shape[0] for r in rows)
    depth, kinds, width = proj_weight.shape
    turned = pltpu.VMEM(kv.shape, BF16)
    half = pltpu.VMEM((count, width), BF16)
    slots = min(SLOTS, (depth - first) // STEP)
    return pl.pallas_call(
        functools.partial(near_kernel, len(rows), first),
        in_specs=[VMEM] * len(rows) + [HBM, VMEM, VMEM],
        out_specs=[VMEM] * 5,
        out_shape=[turned, turned, pltpu.VMEM((2 * count, depth), BF16), half, half],
        scratch_shapes=[
            pltpu.VMEM((2, count, width), F32),
            pltpu.VMEM((slots, STEP, kinds, width), BF16),
            pltpu.SemaphoreType.DMA((slots,)),
        ],
        input_output_aliases={len(rows) + 1: 0, len(rows) + 2: 1},
        compiler_params=pltpu.CompilerParams(vmem_limit_bytes=11 * MIB),
        cost_estimate=pl.CostEstimate(
            flops=2 * count * depth * kinds * width,
            bytes_accessed=4 * depth * kinds * width,
            transcendentals=0,
        ),
        name="project_near",
    )(*rows, in_hbm(proj_weight), pinned(kv), pinned(qg))


def far_kernel(n_rows, rate_ref, place_ref, k0, v0, kv, _, *refs):
    x_refs = refs[:n_rows]
    x_all, k_ref, v_ref, s_ref = refs[n_rows:]
    count, width = k_ref.shape
    gather_rows(x_refs, x_all, count)
    for i, ref in enumerate((k_ref, v_ref)):
        ref[...] = silu(
            jnp.dot(
                x_all[count:],
                kv[:, i * width : (i + 1) * width],
                preferred_element_type=F32,
            )
        )
    for h in range(s_ref.shape[0]):
        cols = slice(h * HD, (h + 1) * HD)
        fade = jnp.exp(-rate_ref[h] * (BLOCK - 1.0 - place_ref[...]))
        k = jnp.concatenate([k0[:, cols], k_ref[:, cols]], 0).astype(F32) * fade
        v = jnp.concatenate([v0[:, cols], v_ref[:, cols]], 0)
        s_ref[h] = lax.dot_general(
            k.astype(BF16), v, (((0,), (0,)), ((), ())), preferred_element_type=F32
        ).astype(BF16)


def project_far(rate, down, k0, v0, kv, x_all, rows):
    count = sum(r.shape[0] for r in rows)
    depth, width = rows[0].shape[1], k0.shape[1]
    half = pltpu.VMEM((count, width), BF16)
    return pl.pallas_call(
        functools.partial(far_kernel, len(rows)),
        in_specs=[SMEM] + [VMEM] * (5 + len(rows)),
        out_specs=[VMEM] * 4,
        out_shape=[
            pltpu.VMEM(x_all.shape, BF16),
            half,
            half,
            jax.ShapeDtypeStruct((rate.shape[0], HD, HD), BF16),
        ],
        input_output_aliases={5: 0},
        compiler_params=pltpu.CompilerParams(vmem_limit_bytes=2 * MIB),
        cost_estimate=pl.CostEstimate(
            flops=4 * count * depth * width, bytes_accessed=4 * depth * width, transcendentals=0
        ),
        name="project_far",
    )(rate, down, k0, v0, pinned(kv), pinned(x_all), *rows)


def block_decay(rate):
    return jnp.exp(jnp.full((HD, HD), -rate * BLOCK, F32))


def carry_kernel(rate_ref, own_ref, came_ref, _, o_ref):
    came = lax.axis_index("seq") > 0
    for h in range(o_ref.shape[0]):
        o_ref[h] = (
            own_ref[h].astype(F32)
            + jnp.where(came, block_decay(rate_ref[h]) * came_ref[h].astype(F32), 0.0)
        ).astype(BF16)


def gates_kernel(x_all, qg, w_hbm, q_ref, g_ref, w_ref, sem):
    copy = pltpu.make_async_copy(w_hbm, w_ref, sem)
    copy.start()
    width = q_ref.shape[1]
    q_ref[...] = silu(jnp.dot(x_all[...], qg[:, :width], preferred_element_type=F32))
    mixed = jnp.dot(x_all[...], qg[:, width:], preferred_element_type=F32)
    g_ref[...] = 1.0 / (1.0 + jnp.exp(-mixed))
    copy.wait()


def gates(x_all, qg, w):
    count, depth = x_all.shape
    width = qg.shape[1] // 2
    return pl.pallas_call(
        gates_kernel,
        in_specs=[VMEM, VMEM, HBM],
        out_specs=[VMEM] * 3,
        out_shape=[
            pltpu.VMEM((count, width), BF16),
            pltpu.VMEM((count, width), F32),
            pltpu.VMEM(w.shape, w.dtype),
        ],
        scratch_shapes=[pltpu.SemaphoreType.DMA],
        compiler_params=pltpu.CompilerParams(vmem_limit_bytes=2 * MIB),
        cost_estimate=pl.CostEstimate(
            flops=4 * count * depth * width, bytes_accessed=8 * depth * width, transcendentals=0
        ),
        name="gates",
    )(pinned(x_all), pinned(qg), in_hbm(w))


def inner_kernel(rate_ref, place_ref, across_ref, q_ref, k0, k1, v0, v1, o_ref):
    diff = place_ref[...] - across_ref[...]
    seen = diff >= 0
    diff = jnp.maximum(diff, 0.0)
    for h in range(o_ref.shape[1] // HD):
        cols = slice(h * HD, (h + 1) * HD)
        k = jnp.concatenate([k0[:, cols], k1[:, cols]], 0)
        v = jnp.concatenate([v0[:, cols], v1[:, cols]], 0)
        scores = lax.dot_general(
            q_ref[:, cols], k, (((1,), (1,)), ((), ())), preferred_element_type=F32
        )
        causal = jnp.where(seen, jnp.exp(-rate_ref[h] * diff), 0.0)
        o_ref[:, cols] = jnp.dot(
            (scores * causal).astype(BF16), v, preferred_element_type=F32
        )


TO_SUM = (3, 7, 1, 2, 5, 6, 0, 4)


def finish_kernel(rate_ref, place_ref, gain_ref, in_ref, q_ref, g_ref, s1, s2, s3, y_ref, z_ref):
    part = in_ref.shape[0] // 8
    block = lax.axis_index("seq")
    for h in range(in_ref.shape[1] // HD):
        cols = slice(h * HD, (h + 1) * HD)
        rate = rate_ref[h]
        fade = block_decay(rate)
        state = jnp.where(block > 0, s1[h].astype(F32), 0.0) + fade * (
            jnp.where(block > 1, s2[h].astype(F32), 0.0)
            + fade * jnp.where(block > 2, s3[h].astype(F32), 0.0)
        )
        high = state.astype(BF16)
        low = (state - high.astype(F32)).astype(BF16)
        q = q_ref[:, cols]
        extra = jnp.dot(q, high, preferred_element_type=F32) + jnp.dot(
            q, low, preferred_element_type=F32
        )
        attn = in_ref[:, cols] + extra * jnp.exp(-rate * (place_ref[...] + 1.0))
        square = jnp.mean(attn * attn, axis=-1, keepdims=True)
        y = (attn * lax.rsqrt(square + 1e-06) * gain_ref[:, cols] * g_ref[:, cols]).astype(BF16)
        for slot, to in enumerate(TO_SUM):
            to_ref, at = (y_ref, to) if to < 4 else (z_ref, to - 4)
            to_ref[at * part : (at + 1) * part, cols] = y[slot * part : (slot + 1) * part]


def small(kernel, n_smem, out, name, *args):
    return pl.pallas_call(
        kernel,
        in_specs=[SMEM] * n_smem + [VMEM] * (len(args) - n_smem),
        out_specs=jax.tree.map(lambda _: VMEM, out),
        out_shape=out,
        compiler_params=pltpu.CompilerParams(vmem_limit_bytes=3 * MIB),
        name=name,
    )(*args)


def out_own_kernel(y_ref, w_ref, o_ref):
    step = 1024
    for at in range(0, o_ref.shape[1], step):
        cols = slice(at, at + step)
        o_ref[:, cols] = jnp.dot(y_ref[...], w_ref[:, cols], preferred_element_type=F32)


def out_own(y, w):
    rows, depth = y.shape
    width = w.shape[1]
    return pl.pallas_call(
        out_own_kernel,
        in_specs=[VMEM] * 2,
        out_specs=VMEM,
        out_shape=pltpu.VMEM((rows, width), F32),
        compiler_params=pltpu.CompilerParams(vmem_limit_bytes=4 * MIB),
        cost_estimate=pl.CostEstimate(
            flops=2 * rows * depth * width, bytes_accessed=2 * depth * width, transcendentals=0
        ),
        name="out_own",
    )(y, pinned(w))


def out_kernel(own_ref, z_ref, u_ref, a_ref, b_ref, c_ref, d_ref):
    rows, width = a_ref.shape
    step = 1024
    for at in range(0, width, step):
        cols = slice(at, at + step)
        total = own_ref[:, cols] + jnp.dot(
            z_ref[...], u_ref[:, cols], preferred_element_type=F32
        )
        for i, ref in enumerate((a_ref, b_ref, c_ref, d_ref)):
            ref[:, cols] = total[i * rows : (i + 1) * rows].astype(ref.dtype)


def out_rows(own, z, u):
    rows, width = own.shape
    send = jax.ShapeDtypeStruct((rows // 4, width), BF16)
    keep = jax.ShapeDtypeStruct((rows // 4, width), F32)
    return pl.pallas_call(
        out_kernel,
        in_specs=[VMEM] * 3,
        out_specs=[VMEM] * 4,
        out_shape=[send, keep, send, keep],
        compiler_params=pltpu.CompilerParams(vmem_limit_bytes=4 * MIB),
        cost_estimate=pl.CostEstimate(
            flops=2 * rows * z.shape[1] * width,
            bytes_accessed=2 * z.shape[1] * width,
            transcendentals=0,
        ),
        name="out_rows",
    )(pinned(own), z, pinned(u))


def paired_device(tokens, proj_weight, out_weight, head_gain, decay_rate):
    rows = tokens.shape[0]
    heads = decay_rate.shape[0]

    cuts = [proj_weight.shape[0] // STEP * part // 8 * STEP for part in (0, 3, 6)]
    w_other = hop(out_weight, CORE)
    first = hop(tokens, FIRST)
    outs = [
        jax.ShapeDtypeStruct(tokens.shape, tokens.dtype),
        pltpu.VMEM((8 * rows, 1), F32),
        pltpu.VMEM((1, 8 * rows), F32),
    ]
    *turned, passed, down, across = prep(0, cuts[1], proj_weight, [], tokens, outs, "prep_a")
    second = hop(passed, SECOND)
    beside = hop(tokens, CORE)
    (first,) = tie([first], [down])
    far = hop(first, SECOND)
    second_beside = hop(first, CORE)
    turned = prep(cuts[1], cuts[2], proj_weight, turned, tokens, [], "prep_b")
    kv, qg, x_all, k0, v0 = project_near(
        [passed, beside, first, second], cuts[2], proj_weight, *turned
    )
    first_beside = hop(second, CORE)
    (far,) = tie([far], [k0])
    far_beside = hop(far, CORE)
    x_all, k1, v1, states = project_far(
        decay_rate, down, k0, v0, kv, x_all, [second_beside, first_beside, far, far_beside]
    )

    came = [
        lax.ppermute(states, "seq", [(i, (i + k) % 4) for i in range(4)]) for k in (1, 2)
    ]
    came.append(lax.ppermute(states, "seq", [(0, 3)]))
    q, g, w_own = gates(x_all, qg, out_weight)
    full = jax.ShapeDtypeStruct((8 * rows, heads * HD), F32)
    inner = small(inner_kernel, 1, full, "inner", decay_rate, down, across, q, k0, k1, v0, v1)
    split = jax.ShapeDtypeStruct((4 * rows, heads * HD), BF16)
    y, y_other = small(
        finish_kernel,
        1,
        [split, split],
        "finish",
        decay_rate, down, head_gain[None, :], inner, q, g, *came,
    )
    z = hop(y_other, CORE)
    a, b, c, d = out_rows(out_own(y, w_own), z, w_other)
    got_a = hop(a, SECOND)
    got_c = hop(c, SECOND)
    got_b = hop((b + got_a.astype(F32)).astype(BF16), FIRST)
    summed = lax.optimization_barrier(d + got_c.astype(F32))
    return (summed + got_b.astype(F32)).astype(BF16)


def solution(mesh):
    paired = mesh.shape["tp"] == 8 and mesh.shape["seq"] == 4
    return jax.shard_map(
        paired_device if paired else general_device,
        mesh=mesh,
        in_specs=(P(("seq", "tp"), None), P(None, None, "tp"), P("tp", None), P("tp"), P("tp")),
        out_specs=P(("seq", "tp"), None),
        check_vma=False,
    )
```

```python
import functools

import jax
import jax.numpy as jnp
from jax import lax
from jax.experimental import pallas as pl
from jax.experimental.pallas import tpu as pltpu
from jax.sharding import PartitionSpec as P

HD = 128
BLOCK = 256
F32, BF16 = jnp.float32, jnp.bfloat16
VMEM = pl.BlockSpec(memory_space=pltpu.VMEM)
SMEM = pl.BlockSpec(memory_space=pltpu.SMEM)
HBM = pl.BlockSpec(memory_space=pl.ANY)
MIB = 1 << 20


def entering(value, axis, combine, identity):
    count, position = (lax.axis_size(axis), lax.axis_index(axis))
    everything = jax.tree.map(
        lambda part, kind: lax.all_gather(part.astype(kind), axis),
        value,
        (jnp.bfloat16, jnp.bfloat16),
    )
    start = jax.tree.map(
        lambda part, zero: jnp.broadcast_to(jnp.asarray(zero, part.dtype), part.shape),
        value,
        identity,
    )

    def turn(k, before):
        reached = k < position
        new = combine(
            before, jax.tree.map(lambda part, own: part[k].astype(own.dtype), everything, value)
        )
        return jax.tree.map(lambda a, b: jnp.where(reached, a, b), new, before)

    return lax.fori_loop(0, count, turn, start)


def attend(q_head, k_head, v_head, rate, start_state):
    count = q_head.shape[0] // BLOCK
    place = jnp.arange(BLOCK).astype(jnp.float32)
    diff = place[:, None] - place[None, :]
    causal = jnp.where(diff >= 0, jnp.exp(-rate * jnp.maximum(diff, 0.0)), 0.0)
    in_decay = jnp.exp(-rate * (place + 1.0))
    out_decay = jnp.exp(-rate * (BLOCK - 1.0 - place))
    block_decay = jnp.exp(-rate * BLOCK)
    q_blocks = q_head.reshape(count, BLOCK, q_head.shape[1])
    k_blocks = k_head.reshape(count, BLOCK, k_head.shape[1])
    v_blocks = v_head.reshape(count, BLOCK, v_head.shape[1])

    def advance(state, block):
        q_blk, k_blk, v_blk = block
        scores = jnp.dot(q_blk, k_blk.T, preferred_element_type=jnp.float32)
        weighted = (scores * causal).astype(jnp.bfloat16)
        inner = jnp.dot(weighted, v_blk, preferred_element_type=jnp.float32)
        carried = (
            jnp.dot(q_blk.astype(jnp.float32), state, precision=lax.Precision.HIGHEST)
            * in_decay[:, None]
        )
        scaled = k_blk.astype(jnp.float32) * out_decay[:, None]
        update = jnp.dot(scaled.T, v_blk.astype(jnp.float32), precision=lax.Precision.HIGHEST)
        return (block_decay * state + update, inner + carried)

    final_state, outputs = lax.scan(advance, start_state, (q_blocks, k_blocks, v_blocks))
    return (outputs.reshape(q_head.shape[0], q_head.shape[1]), final_state)


def general_device(tokens, proj_weight, out_weight, head_gain, decay_rate):
    heads_here = decay_rate.shape[0]
    width = head_gain.shape[0]
    flat = proj_weight.reshape(proj_weight.shape[0], 4 * width)
    mixed = jnp.dot(
        lax.all_gather(tokens, "tp", axis=0, tiled=True), flat, preferred_element_type=jnp.float32
    )
    local_rows = mixed.shape[0]
    q_all = jax.nn.silu(mixed[:, :width]).astype(jnp.bfloat16).reshape(local_rows, heads_here, HD)
    k_all = (
        jax.nn.silu(mixed[:, width : 2 * width])
        .astype(jnp.bfloat16)
        .reshape(local_rows, heads_here, HD)
    )
    v_all = (
        jax.nn.silu(mixed[:, 2 * width : 3 * width])
        .astype(jnp.bfloat16)
        .reshape(local_rows, heads_here, HD)
    )
    gate = mixed[:, 3 * width :].reshape(local_rows, heads_here, HD)
    zero_state = jnp.zeros((HD, HD), jnp.float32)
    outputs, local_states = jax.vmap(attend, in_axes=(1, 1, 1, 0, None), out_axes=(1, 0))(
        q_all, k_all, v_all, decay_rate, zero_state
    )
    zero_states = jnp.zeros((heads_here, HD, HD), jnp.float32)
    span_decay = jnp.exp(-decay_rate * local_rows)

    def combine(earlier, later):
        return (later[1][:, None, None] * earlier[0] + later[0], earlier[1] * later[1])

    incoming, unused = entering(
        (local_states, span_decay), "seq", combine, (zero_states, jnp.ones_like(span_decay))
    )
    place = jnp.arange(local_rows).astype(jnp.float32)
    lift = jnp.exp(-decay_rate[None, :] * (place[:, None] + 1.0))
    extra = jnp.einsum(
        "thd,hde->the", q_all.astype(jnp.float32), incoming, precision=lax.Precision.HIGHEST
    )
    attn = outputs + extra * lift[:, :, None]
    square = jnp.mean(attn * attn, axis=-1, keepdims=True)
    normed = (
        attn
        * lax.rsqrt(square + 1e-06)
        * head_gain.reshape(heads_here, HD)[None]
        * jax.nn.sigmoid(gate)
    )
    joined = normed.astype(jnp.bfloat16).reshape(local_rows, width)
    return lax.psum_scatter(
        jnp.dot(joined, out_weight, preferred_element_type=jnp.float32).astype(jnp.bfloat16),
        "tp",
        scatter_dimension=0,
        tiled=True,
    )


CORE = [(i, i ^ 1) for i in range(8)]
FIRST = [(i, i ^ (4 if i & 1 else 2)) for i in range(8)]
SECOND = [(i, i ^ (2 if i & 1 else 4)) for i in range(8)]


def hop(value, pairs):
    return lax.ppermute(value, "tp", pairs)


STEP = 256
SLOTS = 8


def pinned(value):
    return pltpu.with_memory_space_constraint(value, pltpu.VMEM)


def in_hbm(value):
    return pltpu.with_memory_space_constraint(value, pltpu.HBM)


def chunks(first, count, w_hbm, buf, sem):
    slots, step = buf.shape[:2]

    def copy(i):
        return pltpu.make_async_copy(
            w_hbm.at[pl.ds(first + i * step, step)], buf.at[i % slots], sem.at[i % slots]
        )

    def arriving():
        for i in range(count):
            copy(i).wait()
            yield i, buf[i % slots]
            if i + slots < count:
                copy(i + slots).start()

    for i in range(min(slots, count)):
        copy(i).start()
    return arriving()


def turn(block, at, kv_ref, qg_ref):
    width = block.shape[2]
    turned = jnp.swapaxes(block, 0, 1)
    kv_ref[at, :width] = turned[1]
    kv_ref[at, width:] = turned[2]
    qg_ref[at, :width] = turned[0]
    qg_ref[at, width:] = turned[3]
    return turned


def slot_places(index, shape, axis):
    row = lax.broadcasted_iota(jnp.int32, shape, axis)
    part = shape[axis] // 8
    core = index & 1
    near = jnp.where(core == 0, 2, 4)
    far = 6 - near
    owners = (
        index,
        index ^ 1,
        index ^ near,
        index ^ far,
        index ^ 1 ^ far,
        index ^ 1 ^ near,
        index ^ 6,
        index ^ 7,
    )
    place = row
    for slot, owner in enumerate(owners):
        place = jnp.where(row // part == slot, row + (owner - slot) * part, place)
    return place.astype(F32)


def tie_kernel(*refs):
    pass


def tie(values, others):
    return pl.pallas_call(
        tie_kernel,
        in_specs=[HBM] * (len(values) + len(others)),
        out_specs=[HBM] * len(values),
        out_shape=[jax.ShapeDtypeStruct(v.shape, v.dtype) for v in values],
        input_output_aliases={i: i for i in range(len(values))},
        compiler_params=pltpu.CompilerParams(vmem_limit_bytes=MIB // 4),
        name="tie",
    )(*values, *others)


def prep_kernel(first, last, started, w_hbm, pass_ref, *refs):
    refs = refs[2 * started :]
    kv_ref, qg_ref, *outs = refs[:-3]
    buf, sem, pass_sem = refs[-3:]
    step = buf.shape[1]
    passing = []
    if outs:
        passing = [pltpu.make_async_copy(pass_ref, outs[0], pass_sem)]
    for copy in passing:
        copy.start()
    arriving = chunks(first, (last - first) // step, w_hbm, buf, sem)
    if outs:
        index = lax.axis_index("tp")
        for axis, ref in enumerate(outs[1:]):
            ref[...] = slot_places(index, ref.shape, axis)
    for i, block in arriving:
        turn(block, slice(first + i * step, first + (i + 1) * step), kv_ref, qg_ref)
    for copy in passing:
        copy.wait()


def prep(first, last, proj_weight, turned, passed, outs, name):
    depth, kinds, width = proj_weight.shape
    out = pltpu.VMEM((depth, 2 * width), BF16)
    slots = min(SLOTS, (last - first) // STEP)
    return pl.pallas_call(
        functools.partial(prep_kernel, first, last, bool(turned)),
        in_specs=[HBM, HBM] + [VMEM] * len(turned),
        out_specs=[VMEM] * (2 + len(outs)),
        out_shape=[out, out, *outs],
        scratch_shapes=[
            pltpu.VMEM((slots, STEP, kinds, width), BF16),
            pltpu.SemaphoreType.DMA((slots,)),
            pltpu.SemaphoreType.DMA,
        ],
        input_output_aliases={2 + i: i for i in range(len(turned))},
        compiler_params=pltpu.CompilerParams(vmem_limit_bytes=11 * MIB),
        cost_estimate=pl.CostEstimate(
            flops=0, bytes_accessed=4 * (last - first) * kinds * width, transcendentals=0
        ),
        name=name,
    )(in_hbm(proj_weight), in_hbm(passed), *map(pinned, turned))


def gather_rows(x_refs, x_all, at):
    for ref in x_refs:
        x_all[at : at + ref.shape[0], :] = ref[...]
        at += ref.shape[0]


def silu(mixed):
    return (mixed / (1.0 + jnp.exp(-mixed))).astype(BF16)


def near_kernel(n_rows, first, *refs):
    x_refs = refs[:n_rows]
    w_hbm, _, _, kv, qg, x_all, k_ref, v_ref, total, buf, sem = refs[n_rows:]
    step, (count, width) = buf.shape[1], k_ref.shape
    depth = kv.shape[0]
    arriving = chunks(first, (depth - first) // step, w_hbm, buf, sem)
    gather_rows(x_refs, x_all, 0)
    for i in range(2):
        total[i] = jnp.dot(
            x_all[:count, :first],
            kv[:first, i * width : (i + 1) * width],
            preferred_element_type=F32,
        )
    for c, block in arriving:
        at = first + c * step
        turned = turn(block, slice(at, at + step), kv, qg)
        for i in range(2):
            total[i] += jnp.dot(
                x_all[:count, at : at + step], turned[1 + i], preferred_element_type=F32
            )
    k_ref[...] = silu(total[0])
    v_ref[...] = silu(total[1])


def project_near(rows, first, proj_weight, kv, qg):
    count = sum(r.shape[0] for r in rows)
    depth, kinds, width = proj_weight.shape
    turned = pltpu.VMEM(kv.shape, BF16)
    half = pltpu.VMEM((count, width), BF16)
    slots = min(SLOTS, (depth - first) // STEP)
    return pl.pallas_call(
        functools.partial(near_kernel, len(rows), first),
        in_specs=[VMEM] * len(rows) + [HBM, VMEM, VMEM],
        out_specs=[VMEM] * 5,
        out_shape=[turned, turned, pltpu.VMEM((2 * count, depth), BF16), half, half],
        scratch_shapes=[
            pltpu.VMEM((2, count, width), F32),
            pltpu.VMEM((slots, STEP, kinds, width), BF16),
            pltpu.SemaphoreType.DMA((slots,)),
        ],
        input_output_aliases={len(rows) + 1: 0, len(rows) + 2: 1},
        compiler_params=pltpu.CompilerParams(vmem_limit_bytes=11 * MIB),
        cost_estimate=pl.CostEstimate(
            flops=2 * count * depth * kinds * width,
            bytes_accessed=4 * depth * kinds * width,
            transcendentals=0,
        ),
        name="project_near",
    )(*rows, in_hbm(proj_weight), pinned(kv), pinned(qg))


def far_kernel(n_rows, rate_ref, place_ref, k0, v0, kv, _, *refs):
    x_refs = refs[:n_rows]
    x_all, k_ref, v_ref, s_ref = refs[n_rows:]
    count, width = k_ref.shape
    gather_rows(x_refs, x_all, count)
    for i, ref in enumerate((k_ref, v_ref)):
        ref[...] = silu(
            jnp.dot(
                x_all[count:],
                kv[:, i * width : (i + 1) * width],
                preferred_element_type=F32,
            )
        )
    for h in range(s_ref.shape[0]):
        cols = slice(h * HD, (h + 1) * HD)
        fade = jnp.exp(-rate_ref[h] * (BLOCK - 1.0 - place_ref[...]))
        k = jnp.concatenate([k0[:, cols], k_ref[:, cols]], 0).astype(F32) * fade
        v = jnp.concatenate([v0[:, cols], v_ref[:, cols]], 0)
        s_ref[h] = lax.dot_general(
            k.astype(BF16), v, (((0,), (0,)), ((), ())), preferred_element_type=F32
        ).astype(BF16)


def project_far(rate, down, k0, v0, kv, x_all, rows):
    count = sum(r.shape[0] for r in rows)
    depth, width = rows[0].shape[1], k0.shape[1]
    half = pltpu.VMEM((count, width), BF16)
    return pl.pallas_call(
        functools.partial(far_kernel, len(rows)),
        in_specs=[SMEM] + [VMEM] * (5 + len(rows)),
        out_specs=[VMEM] * 4,
        out_shape=[
            pltpu.VMEM(x_all.shape, BF16),
            half,
            half,
            jax.ShapeDtypeStruct((rate.shape[0], HD, HD), BF16),
        ],
        input_output_aliases={5: 0},
        compiler_params=pltpu.CompilerParams(vmem_limit_bytes=2 * MIB),
        cost_estimate=pl.CostEstimate(
            flops=4 * count * depth * width, bytes_accessed=4 * depth * width, transcendentals=0
        ),
        name="project_far",
    )(rate, down, k0, v0, pinned(kv), pinned(x_all), *rows)


def block_decay(rate):
    return jnp.exp(jnp.full((HD, HD), -rate * BLOCK, F32))


def carry_kernel(rate_ref, own_ref, came_ref, _, o_ref):
    came = lax.axis_index("seq") > 0
    for h in range(o_ref.shape[0]):
        o_ref[h] = (
            own_ref[h].astype(F32)
            + jnp.where(came, block_decay(rate_ref[h]) * came_ref[h].astype(F32), 0.0)
        ).astype(BF16)


def early_kernel(_, qg, x_all, q_ref):
    count, width = q_ref.shape
    q_ref[...] = silu(jnp.dot(x_all[:count], qg[:, :width], preferred_element_type=F32))


def early(x_all, qg):
    count, depth = x_all.shape[0] // 2, x_all.shape[1]
    width = qg.shape[1] // 2

    return pl.pallas_call(
        early_kernel,
        in_specs=[VMEM, VMEM],
        out_specs=[VMEM, VMEM],
        out_shape=[pltpu.VMEM(x_all.shape, BF16), pltpu.VMEM((count, width), BF16)],
        input_output_aliases={0: 0},
        compiler_params=pltpu.CompilerParams(vmem_limit_bytes=2 * MIB),
        cost_estimate=pl.CostEstimate(
            flops=2 * count * depth * width, bytes_accessed=2 * depth * width, transcendentals=0
        ),
        name="early",
    )(pinned(x_all), pinned(qg))


def gates_kernel(x_all, qg, w_hbm, q_ref, g_ref, w_ref, sem):
    copy = pltpu.make_async_copy(w_hbm, w_ref, sem)
    copy.start()
    count, width = q_ref.shape
    q_ref[...] = silu(jnp.dot(x_all[count:], qg[:, :width], preferred_element_type=F32))
    mixed = jnp.dot(x_all[...], qg[:, width:], preferred_element_type=F32)
    g_ref[...] = 1.0 / (1.0 + jnp.exp(-mixed))
    copy.wait()


def gates(x_all, qg, w):
    count, depth = x_all.shape
    width = qg.shape[1] // 2
    return pl.pallas_call(
        gates_kernel,
        in_specs=[VMEM, VMEM, HBM],
        out_specs=[VMEM] * 3,
        out_shape=[
            pltpu.VMEM((count // 2, width), BF16),
            pltpu.VMEM((count, width), F32),
            pltpu.VMEM(w.shape, w.dtype),
        ],
        scratch_shapes=[pltpu.SemaphoreType.DMA],
        compiler_params=pltpu.CompilerParams(vmem_limit_bytes=2 * MIB),
        cost_estimate=pl.CostEstimate(
            flops=3 * count * depth * width, bytes_accessed=8 * depth * width, transcendentals=0
        ),
        name="gates",
    )(pinned(x_all), pinned(qg), in_hbm(w))


def inner_kernel(rate_ref, place_ref, across_ref, q0, q1, k0, k1, v0, v1, o_ref):
    diff = place_ref[...] - across_ref[...]
    seen = diff >= 0
    diff = jnp.maximum(diff, 0.0)
    for h in range(o_ref.shape[1] // HD):
        cols = slice(h * HD, (h + 1) * HD)
        q = jnp.concatenate([q0[:, cols], q1[:, cols]], 0)
        k = jnp.concatenate([k0[:, cols], k1[:, cols]], 0)
        v = jnp.concatenate([v0[:, cols], v1[:, cols]], 0)
        scores = lax.dot_general(q, k, (((1,), (1,)), ((), ())), preferred_element_type=F32)
        causal = jnp.where(seen, jnp.exp(-rate_ref[h] * diff), 0.0)
        o_ref[:, cols] = jnp.dot(
            (scores * causal).astype(BF16), v, preferred_element_type=F32
        )


TO_SUM = (3, 7, 1, 2, 5, 6, 0, 4)


def finish_kernel(rate_ref, place_ref, gain_ref, in_ref, q0, q1, g_ref, s1, s2, s3, y_ref, z_ref):
    part = in_ref.shape[0] // 8
    block = lax.axis_index("seq")
    for h in range(in_ref.shape[1] // HD):
        cols = slice(h * HD, (h + 1) * HD)
        rate = rate_ref[h]
        fade = block_decay(rate)
        state = jnp.where(block > 0, s1[h].astype(F32), 0.0) + fade * (
            jnp.where(block > 1, s2[h].astype(F32), 0.0)
            + fade * jnp.where(block > 2, s3[h].astype(F32), 0.0)
        )
        high = state.astype(BF16)
        low = (state - high.astype(F32)).astype(BF16)
        q = jnp.concatenate([q0[:, cols], q1[:, cols]], 0)
        extra = jnp.dot(q, high, preferred_element_type=F32) + jnp.dot(
            q, low, preferred_element_type=F32
        )
        attn = in_ref[:, cols] + extra * jnp.exp(-rate * (place_ref[...] + 1.0))
        square = jnp.mean(attn * attn, axis=-1, keepdims=True)
        y = (attn * lax.rsqrt(square + 1e-06) * gain_ref[:, cols] * g_ref[:, cols]).astype(BF16)
        for slot, to in enumerate(TO_SUM):
            to_ref, at = (y_ref, to) if to < 4 else (z_ref, to - 4)
            to_ref[at * part : (at + 1) * part, cols] = y[slot * part : (slot + 1) * part]


def small(kernel, n_smem, out, name, *args):
    return pl.pallas_call(
        kernel,
        in_specs=[SMEM] * n_smem + [VMEM] * (len(args) - n_smem),
        out_specs=jax.tree.map(lambda _: VMEM, out),
        out_shape=out,
        compiler_params=pltpu.CompilerParams(vmem_limit_bytes=3 * MIB),
        name=name,
    )(*args)


def out_own_kernel(y_ref, w_ref, o_ref):
    step = 1024
    for at in range(0, o_ref.shape[1], step):
        cols = slice(at, at + step)
        o_ref[:, cols] = jnp.dot(y_ref[...], w_ref[:, cols], preferred_element_type=F32)


def out_own(y, w):
    rows, depth = y.shape
    width = w.shape[1]
    return pl.pallas_call(
        out_own_kernel,
        in_specs=[VMEM] * 2,
        out_specs=VMEM,
        out_shape=pltpu.VMEM((rows, width), F32),
        compiler_params=pltpu.CompilerParams(vmem_limit_bytes=4 * MIB),
        cost_estimate=pl.CostEstimate(
            flops=2 * rows * depth * width, bytes_accessed=2 * depth * width, transcendentals=0
        ),
        name="out_own",
    )(y, pinned(w))


def out_kernel(own_ref, z_ref, u_ref, a_ref, b_ref, c_ref, d_ref):
    rows, width = a_ref.shape
    step = 1024
    for at in range(0, width, step):
        cols = slice(at, at + step)
        total = own_ref[:, cols] + jnp.dot(
            z_ref[...], u_ref[:, cols], preferred_element_type=F32
        )
        for i, ref in enumerate((a_ref, b_ref, c_ref, d_ref)):
            ref[:, cols] = total[i * rows : (i + 1) * rows].astype(ref.dtype)


def out_rows(own, z, u):
    rows, width = own.shape
    send = jax.ShapeDtypeStruct((rows // 4, width), BF16)
    keep = jax.ShapeDtypeStruct((rows // 4, width), F32)
    return pl.pallas_call(
        out_kernel,
        in_specs=[VMEM] * 3,
        out_specs=[VMEM] * 4,
        out_shape=[send, keep, send, keep],
        compiler_params=pltpu.CompilerParams(vmem_limit_bytes=4 * MIB),
        cost_estimate=pl.CostEstimate(
            flops=2 * rows * z.shape[1] * width,
            bytes_accessed=2 * z.shape[1] * width,
            transcendentals=0,
        ),
        name="out_rows",
    )(pinned(own), z, pinned(u))


def paired_device(tokens, proj_weight, out_weight, head_gain, decay_rate):
    rows = tokens.shape[0]
    heads = decay_rate.shape[0]

    cuts = [proj_weight.shape[0] // STEP * part // 8 * STEP for part in (0, 3, 6)]
    w_other = hop(out_weight, CORE)
    first = hop(tokens, FIRST)
    outs = [
        jax.ShapeDtypeStruct(tokens.shape, tokens.dtype),
        pltpu.VMEM((8 * rows, 1), F32),
        pltpu.VMEM((1, 8 * rows), F32),
    ]
    *turned, passed, down, across = prep(0, cuts[1], proj_weight, [], tokens, outs, "prep_a")
    second = hop(passed, SECOND)
    beside = hop(tokens, CORE)
    (first,) = tie([first], [down])
    far = hop(first, SECOND)
    second_beside = hop(first, CORE)
    turned = prep(cuts[1], cuts[2], proj_weight, turned, tokens, [], "prep_b")
    kv, qg, x_all, k0, v0 = project_near(
        [passed, beside, first, second], cuts[2], proj_weight, *turned
    )
    first_beside = hop(second, CORE)
    (far,) = tie([far], [k0])
    far_beside = hop(far, CORE)
    x_all, q0 = early(x_all, qg)
    x_all, k1, v1, states = project_far(
        decay_rate, down, k0, v0, kv, x_all, [second_beside, first_beside, far, far_beside]
    )

    came = [
        lax.ppermute(states, "seq", [(i, (i + 1) % 4) for i in range(4)]),
        lax.ppermute(states, "seq", [(0, 2), (1, 3)]),
    ]
    came.append(lax.ppermute(states, "seq", [(0, 3)]))
    q1, g, w_own = gates(x_all, qg, out_weight)
    full = jax.ShapeDtypeStruct((8 * rows, heads * HD), F32)
    inner = small(inner_kernel, 1, full, "inner", decay_rate, down, across, q0, q1, k0, k1, v0, v1)
    split = jax.ShapeDtypeStruct((4 * rows, heads * HD), BF16)
    y, y_other = small(
        finish_kernel,
        1,
        [split, split],
        "finish",
        decay_rate, down, head_gain[None, :], inner, q0, q1, g, *came,
    )
    z = hop(y_other, CORE)
    a, b, c, d = out_rows(out_own(y, w_own), z, w_other)
    got_a = hop(a, SECOND)
    got_c = hop(c, SECOND)
    got_b = hop((b + got_a.astype(F32)).astype(BF16), FIRST)
    summed = lax.optimization_barrier(d + got_c.astype(F32))
    return (summed + got_b.astype(F32)).astype(BF16)


def solution(mesh):
    paired = mesh.shape["tp"] == 8 and mesh.shape["seq"] == 4
    return jax.shard_map(
        paired_device if paired else general_device,
        mesh=mesh,
        in_specs=(P(("seq", "tp"), None), P(None, None, "tp"), P("tp", None), P("tp"), P("tp")),
        out_specs=P(("seq", "tp"), None),
        check_vma=False,
    )
```

```python
import functools

import jax
import jax.numpy as jnp
from jax import lax
from jax.experimental import pallas as pl
from jax.experimental.pallas import tpu as pltpu
from jax.sharding import PartitionSpec as P

HD = 128
BLOCK = 256
F32, BF16 = jnp.float32, jnp.bfloat16
VMEM = pl.BlockSpec(memory_space=pltpu.VMEM)
SMEM = pl.BlockSpec(memory_space=pltpu.SMEM)
HBM = pl.BlockSpec(memory_space=pl.ANY)
MIB = 1 << 20


def entering(value, axis, combine, identity):
    count, position = (lax.axis_size(axis), lax.axis_index(axis))
    everything = jax.tree.map(
        lambda part, kind: lax.all_gather(part.astype(kind), axis),
        value,
        (jnp.bfloat16, jnp.bfloat16),
    )
    start = jax.tree.map(
        lambda part, zero: jnp.broadcast_to(jnp.asarray(zero, part.dtype), part.shape),
        value,
        identity,
    )

    def turn(k, before):
        reached = k < position
        new = combine(
            before, jax.tree.map(lambda part, own: part[k].astype(own.dtype), everything, value)
        )
        return jax.tree.map(lambda a, b: jnp.where(reached, a, b), new, before)

    return lax.fori_loop(0, count, turn, start)


def attend(q_head, k_head, v_head, rate, start_state):
    count = q_head.shape[0] // BLOCK
    place = jnp.arange(BLOCK).astype(jnp.float32)
    diff = place[:, None] - place[None, :]
    causal = jnp.where(diff >= 0, jnp.exp(-rate * jnp.maximum(diff, 0.0)), 0.0)
    in_decay = jnp.exp(-rate * (place + 1.0))
    out_decay = jnp.exp(-rate * (BLOCK - 1.0 - place))
    block_decay = jnp.exp(-rate * BLOCK)
    q_blocks = q_head.reshape(count, BLOCK, q_head.shape[1])
    k_blocks = k_head.reshape(count, BLOCK, k_head.shape[1])
    v_blocks = v_head.reshape(count, BLOCK, v_head.shape[1])

    def advance(state, block):
        q_blk, k_blk, v_blk = block
        scores = jnp.dot(q_blk, k_blk.T, preferred_element_type=jnp.float32)
        weighted = (scores * causal).astype(jnp.bfloat16)
        inner = jnp.dot(weighted, v_blk, preferred_element_type=jnp.float32)
        carried = (
            jnp.dot(q_blk.astype(jnp.float32), state, precision=lax.Precision.HIGHEST)
            * in_decay[:, None]
        )
        scaled = k_blk.astype(jnp.float32) * out_decay[:, None]
        update = jnp.dot(scaled.T, v_blk.astype(jnp.float32), precision=lax.Precision.HIGHEST)
        return (block_decay * state + update, inner + carried)

    final_state, outputs = lax.scan(advance, start_state, (q_blocks, k_blocks, v_blocks))
    return (outputs.reshape(q_head.shape[0], q_head.shape[1]), final_state)


def general_device(tokens, proj_weight, out_weight, head_gain, decay_rate):
    heads_here = decay_rate.shape[0]
    width = head_gain.shape[0]
    flat = proj_weight.reshape(proj_weight.shape[0], 4 * width)
    mixed = jnp.dot(
        lax.all_gather(tokens, "tp", axis=0, tiled=True), flat, preferred_element_type=jnp.float32
    )
    local_rows = mixed.shape[0]
    q_all = jax.nn.silu(mixed[:, :width]).astype(jnp.bfloat16).reshape(local_rows, heads_here, HD)
    k_all = (
        jax.nn.silu(mixed[:, width : 2 * width])
        .astype(jnp.bfloat16)
        .reshape(local_rows, heads_here, HD)
    )
    v_all = (
        jax.nn.silu(mixed[:, 2 * width : 3 * width])
        .astype(jnp.bfloat16)
        .reshape(local_rows, heads_here, HD)
    )
    gate = mixed[:, 3 * width :].reshape(local_rows, heads_here, HD)
    zero_state = jnp.zeros((HD, HD), jnp.float32)
    outputs, local_states = jax.vmap(attend, in_axes=(1, 1, 1, 0, None), out_axes=(1, 0))(
        q_all, k_all, v_all, decay_rate, zero_state
    )
    zero_states = jnp.zeros((heads_here, HD, HD), jnp.float32)
    span_decay = jnp.exp(-decay_rate * local_rows)

    def combine(earlier, later):
        return (later[1][:, None, None] * earlier[0] + later[0], earlier[1] * later[1])

    incoming, unused = entering(
        (local_states, span_decay), "seq", combine, (zero_states, jnp.ones_like(span_decay))
    )
    place = jnp.arange(local_rows).astype(jnp.float32)
    lift = jnp.exp(-decay_rate[None, :] * (place[:, None] + 1.0))
    extra = jnp.einsum(
        "thd,hde->the", q_all.astype(jnp.float32), incoming, precision=lax.Precision.HIGHEST
    )
    attn = outputs + extra * lift[:, :, None]
    square = jnp.mean(attn * attn, axis=-1, keepdims=True)
    normed = (
        attn
        * lax.rsqrt(square + 1e-06)
        * head_gain.reshape(heads_here, HD)[None]
        * jax.nn.sigmoid(gate)
    )
    joined = normed.astype(jnp.bfloat16).reshape(local_rows, width)
    return lax.psum_scatter(
        jnp.dot(joined, out_weight, preferred_element_type=jnp.float32).astype(jnp.bfloat16),
        "tp",
        scatter_dimension=0,
        tiled=True,
    )


CORE = [(i, i ^ 1) for i in range(8)]
FIRST = [(i, i ^ (4 if i & 1 else 2)) for i in range(8)]
SECOND = [(i, i ^ (2 if i & 1 else 4)) for i in range(8)]


def hop(value, pairs):
    return lax.ppermute(value, "tp", pairs)


STEP = 256
SLOTS = 8


def pinned(value):
    return pltpu.with_memory_space_constraint(value, pltpu.VMEM)


def in_hbm(value):
    return pltpu.with_memory_space_constraint(value, pltpu.HBM)


def chunks(first, count, w_hbm, buf, sem):
    slots, step = buf.shape[:2]

    def copy(i):
        return pltpu.make_async_copy(
            w_hbm.at[pl.ds(first + i * step, step)], buf.at[i % slots], sem.at[i % slots]
        )

    def arriving():
        for i in range(count):
            copy(i).wait()
            yield i, buf[i % slots]
            if i + slots < count:
                copy(i + slots).start()

    for i in range(min(slots, count)):
        copy(i).start()
    return arriving()


def turn(block, at, kv_ref, qg_ref):
    width = block.shape[2]
    turned = jnp.swapaxes(block, 0, 1)
    kv_ref[at, :width] = turned[1]
    kv_ref[at, width:] = turned[2]
    qg_ref[at, :width] = turned[0]
    qg_ref[at, width:] = turned[3]
    return turned


def slot_places(index, shape, axis):
    row = lax.broadcasted_iota(jnp.int32, shape, axis)
    part = shape[axis] // 8
    core = index & 1
    near = jnp.where(core == 0, 2, 4)
    far = 6 - near
    owners = (
        index,
        index ^ 1,
        index ^ near,
        index ^ far,
        index ^ 1 ^ far,
        index ^ 1 ^ near,
        index ^ 6,
        index ^ 7,
    )
    place = row
    for slot, owner in enumerate(owners):
        place = jnp.where(row // part == slot, row + (owner - slot) * part, place)
    return place.astype(F32)


def tie_kernel(*refs):
    pass


def tie(values, others):
    return pl.pallas_call(
        tie_kernel,
        in_specs=[HBM] * (len(values) + len(others)),
        out_specs=[HBM] * len(values),
        out_shape=[jax.ShapeDtypeStruct(v.shape, v.dtype) for v in values],
        input_output_aliases={i: i for i in range(len(values))},
        compiler_params=pltpu.CompilerParams(vmem_limit_bytes=MIB // 4),
        name="tie",
    )(*values, *others)


def prep_kernel(first, last, started, w_hbm, pass_ref, *refs):
    refs = refs[2 * started :]
    kv_ref, qg_ref, *outs = refs[:-3]
    buf, sem, pass_sem = refs[-3:]
    step = buf.shape[1]
    passing = []
    if outs:
        passing = [pltpu.make_async_copy(pass_ref, outs[0], pass_sem)]
    for copy in passing:
        copy.start()
    arriving = chunks(first, (last - first) // step, w_hbm, buf, sem)
    if outs:
        index = lax.axis_index("tp")
        for axis, ref in enumerate(outs[1:]):
            ref[...] = slot_places(index, ref.shape, axis)
    for i, block in arriving:
        turn(block, slice(first + i * step, first + (i + 1) * step), kv_ref, qg_ref)
    for copy in passing:
        copy.wait()


def prep(first, last, proj_weight, turned, passed, outs, name):
    depth, kinds, width = proj_weight.shape
    out = pltpu.VMEM((depth, 2 * width), BF16)
    slots = min(SLOTS, (last - first) // STEP)
    return pl.pallas_call(
        functools.partial(prep_kernel, first, last, bool(turned)),
        in_specs=[HBM, HBM] + [VMEM] * len(turned),
        out_specs=[VMEM] * (2 + len(outs)),
        out_shape=[out, out, *outs],
        scratch_shapes=[
            pltpu.VMEM((slots, STEP, kinds, width), BF16),
            pltpu.SemaphoreType.DMA((slots,)),
            pltpu.SemaphoreType.DMA,
        ],
        input_output_aliases={2 + i: i for i in range(len(turned))},
        compiler_params=pltpu.CompilerParams(vmem_limit_bytes=11 * MIB),
        cost_estimate=pl.CostEstimate(
            flops=0, bytes_accessed=4 * (last - first) * kinds * width, transcendentals=0
        ),
        name=name,
    )(in_hbm(proj_weight), in_hbm(passed), *map(pinned, turned))


def gather_rows(x_refs, x_all, at):
    for ref in x_refs:
        x_all[at : at + ref.shape[0], :] = ref[...]
        at += ref.shape[0]


def silu(mixed):
    return (mixed / (1.0 + jnp.exp(-mixed))).astype(BF16)


def near_kernel(n_rows, first, *refs):
    x_refs = refs[:n_rows]
    w_hbm, _, _, kv, qg, x_all, k_ref, v_ref, total, buf, sem = refs[n_rows:]
    step, (count, width) = buf.shape[1], k_ref.shape
    depth = kv.shape[0]
    arriving = chunks(first, (depth - first) // step, w_hbm, buf, sem)
    gather_rows(x_refs, x_all, 0)
    for i in range(2):
        total[i] = jnp.dot(
            x_all[:count, :first],
            kv[:first, i * width : (i + 1) * width],
            preferred_element_type=F32,
        )
    for c, block in arriving:
        at = first + c * step
        turned = turn(block, slice(at, at + step), kv, qg)
        for i in range(2):
            total[i] += jnp.dot(
                x_all[:count, at : at + step], turned[1 + i], preferred_element_type=F32
            )
    k_ref[...] = silu(total[0])
    v_ref[...] = silu(total[1])


def project_near(rows, first, proj_weight, kv, qg):
    count = sum(r.shape[0] for r in rows)
    depth, kinds, width = proj_weight.shape
    turned = pltpu.VMEM(kv.shape, BF16)
    half = pltpu.VMEM((count, width), BF16)
    slots = min(SLOTS, (depth - first) // STEP)
    return pl.pallas_call(
        functools.partial(near_kernel, len(rows), first),
        in_specs=[VMEM] * len(rows) + [HBM, VMEM, VMEM],
        out_specs=[VMEM] * 5,
        out_shape=[turned, turned, pltpu.VMEM((2 * count, depth), BF16), half, half],
        scratch_shapes=[
            pltpu.VMEM((2, count, width), F32),
            pltpu.VMEM((slots, STEP, kinds, width), BF16),
            pltpu.SemaphoreType.DMA((slots,)),
        ],
        input_output_aliases={len(rows) + 1: 0, len(rows) + 2: 1},
        compiler_params=pltpu.CompilerParams(vmem_limit_bytes=11 * MIB),
        cost_estimate=pl.CostEstimate(
            flops=2 * count * depth * kinds * width,
            bytes_accessed=4 * depth * kinds * width,
            transcendentals=0,
        ),
        name="project_near",
    )(*rows, in_hbm(proj_weight), pinned(kv), pinned(qg))


def far_kernel(n_rows, rate_ref, place_ref, k0, v0, kv, _, *refs):
    x_refs = refs[:n_rows]
    x_all, k_ref, v_ref, s_ref = refs[n_rows:]
    count, width = k_ref.shape
    gather_rows(x_refs, x_all, count)
    for i, ref in enumerate((k_ref, v_ref)):
        ref[...] = silu(
            jnp.dot(
                x_all[count:],
                kv[:, i * width : (i + 1) * width],
                preferred_element_type=F32,
            )
        )
    for h in range(s_ref.shape[0]):
        cols = slice(h * HD, (h + 1) * HD)
        fade = jnp.exp(-rate_ref[h] * (BLOCK - 1.0 - place_ref[...]))
        k = jnp.concatenate([k0[:, cols], k_ref[:, cols]], 0).astype(F32) * fade
        v = jnp.concatenate([v0[:, cols], v_ref[:, cols]], 0)
        s_ref[h] = lax.dot_general(
            k.astype(BF16), v, (((0,), (0,)), ((), ())), preferred_element_type=F32
        ).astype(BF16)


def project_far(rate, down, k0, v0, kv, x_all, rows):
    count = sum(r.shape[0] for r in rows)
    depth, width = rows[0].shape[1], k0.shape[1]
    half = pltpu.VMEM((count, width), BF16)
    return pl.pallas_call(
        functools.partial(far_kernel, len(rows)),
        in_specs=[SMEM] + [VMEM] * (5 + len(rows)),
        out_specs=[VMEM] * 4,
        out_shape=[
            pltpu.VMEM(x_all.shape, BF16),
            half,
            half,
            jax.ShapeDtypeStruct((rate.shape[0], HD, HD), BF16),
        ],
        input_output_aliases={5: 0},
        compiler_params=pltpu.CompilerParams(vmem_limit_bytes=2 * MIB),
        cost_estimate=pl.CostEstimate(
            flops=4 * count * depth * width, bytes_accessed=4 * depth * width, transcendentals=0
        ),
        name="project_far",
    )(rate, down, k0, v0, pinned(kv), pinned(x_all), *rows)


def block_decay(rate):
    return jnp.exp(jnp.full((HD, HD), -rate * BLOCK, F32))


def carry_kernel(rate_ref, own_ref, came_ref, _, o_ref):
    came = lax.axis_index("seq") > 0
    for h in range(o_ref.shape[0]):
        o_ref[h] = (
            own_ref[h].astype(F32)
            + jnp.where(came, block_decay(rate_ref[h]) * came_ref[h].astype(F32), 0.0)
        ).astype(BF16)


def early_kernel(_, qg, x_all, q_ref):
    count, width = q_ref.shape
    q_ref[...] = silu(jnp.dot(x_all[:count], qg[:, :width], preferred_element_type=F32))


def early(x_all, qg):
    count, depth = x_all.shape[0] // 2, x_all.shape[1]
    width = qg.shape[1] // 2

    return pl.pallas_call(
        early_kernel,
        in_specs=[VMEM, VMEM],
        out_specs=[VMEM, VMEM],
        out_shape=[pltpu.VMEM(x_all.shape, BF16), pltpu.VMEM((count, width), BF16)],
        input_output_aliases={0: 0},
        compiler_params=pltpu.CompilerParams(vmem_limit_bytes=2 * MIB),
        cost_estimate=pl.CostEstimate(
            flops=2 * count * depth * width, bytes_accessed=2 * depth * width, transcendentals=0
        ),
        name="early",
    )(pinned(x_all), pinned(qg))


def gates_kernel(x_all, qg, w_hbm, q_ref, g_ref, w_ref, sem):
    copy = pltpu.make_async_copy(w_hbm, w_ref, sem)
    copy.start()
    count, width = q_ref.shape
    q_ref[...] = silu(jnp.dot(x_all[count:], qg[:, :width], preferred_element_type=F32))
    mixed = jnp.dot(x_all[...], qg[:, width:], preferred_element_type=F32)
    g_ref[...] = 1.0 / (1.0 + jnp.exp(-mixed))
    copy.wait()


def gates(x_all, qg, w):
    count, depth = x_all.shape
    width = qg.shape[1] // 2
    return pl.pallas_call(
        gates_kernel,
        in_specs=[VMEM, VMEM, HBM],
        out_specs=[VMEM] * 3,
        out_shape=[
            pltpu.VMEM((count // 2, width), BF16),
            pltpu.VMEM((count, width), F32),
            pltpu.VMEM(w.shape, w.dtype),
        ],
        scratch_shapes=[pltpu.SemaphoreType.DMA],
        compiler_params=pltpu.CompilerParams(vmem_limit_bytes=2 * MIB),
        cost_estimate=pl.CostEstimate(
            flops=3 * count * depth * width, bytes_accessed=8 * depth * width, transcendentals=0
        ),
        name="gates",
    )(pinned(x_all), pinned(qg), in_hbm(w))


def inner_kernel(rate_ref, place_ref, across_ref, q0, q1, k0, k1, v0, v1, o_ref):
    diff = place_ref[...] - across_ref[...]
    seen = diff >= 0
    diff = jnp.maximum(diff, 0.0)
    for h in range(o_ref.shape[1] // HD):
        cols = slice(h * HD, (h + 1) * HD)
        q = jnp.concatenate([q0[:, cols], q1[:, cols]], 0)
        k = jnp.concatenate([k0[:, cols], k1[:, cols]], 0)
        v = jnp.concatenate([v0[:, cols], v1[:, cols]], 0)
        scores = lax.dot_general(q, k, (((1,), (1,)), ((), ())), preferred_element_type=F32)
        causal = jnp.where(seen, jnp.exp(-rate_ref[h] * diff), 0.0)
        o_ref[:, cols] = jnp.dot(
            (scores * causal).astype(BF16), v, preferred_element_type=F32
        )


TO_SUM = (3, 7, 1, 2, 5, 6, 0, 4)


def finish_kernel(rate_ref, place_ref, gain_ref, in_ref, q0, q1, g_ref, s1, s2, s3, y_ref, z_ref):
    part = in_ref.shape[0] // 8
    block = lax.axis_index("seq")
    for h in range(in_ref.shape[1] // HD):
        cols = slice(h * HD, (h + 1) * HD)
        rate = rate_ref[h]
        fade = block_decay(rate)
        state = jnp.where(block > 0, s1[h].astype(F32), 0.0) + fade * (
            jnp.where(block > 1, s2[h].astype(F32), 0.0)
            + fade * jnp.where(block > 2, s3[h].astype(F32), 0.0)
        )
        high = state.astype(BF16)
        low = (state - high.astype(F32)).astype(BF16)
        q = jnp.concatenate([q0[:, cols], q1[:, cols]], 0)
        extra = jnp.dot(q, high, preferred_element_type=F32) + jnp.dot(
            q, low, preferred_element_type=F32
        )
        attn = in_ref[:, cols] + extra * jnp.exp(-rate * (place_ref[...] + 1.0))
        square = jnp.mean(attn * attn, axis=-1, keepdims=True)
        y = (attn * lax.rsqrt(square + 1e-06) * gain_ref[:, cols] * g_ref[:, cols]).astype(BF16)
        for slot, to in enumerate(TO_SUM):
            to_ref, at = (y_ref, to) if to < 4 else (z_ref, to - 4)
            to_ref[at * part : (at + 1) * part, cols] = y[slot * part : (slot + 1) * part]


def small(kernel, n_smem, out, name, *args):
    return pl.pallas_call(
        kernel,
        in_specs=[SMEM] * n_smem + [VMEM] * (len(args) - n_smem),
        out_specs=jax.tree.map(lambda _: VMEM, out),
        out_shape=out,
        compiler_params=pltpu.CompilerParams(vmem_limit_bytes=3 * MIB),
        name=name,
    )(*args)


def out_own_kernel(y_ref, w_ref, o_ref):
    step = 1024
    for at in range(0, o_ref.shape[1], step):
        cols = slice(at, at + step)
        o_ref[:, cols] = jnp.dot(y_ref[...], w_ref[:, cols], preferred_element_type=F32)


def out_own(y, w):
    rows, depth = y.shape
    width = w.shape[1]
    return pl.pallas_call(
        out_own_kernel,
        in_specs=[VMEM] * 2,
        out_specs=VMEM,
        out_shape=pltpu.VMEM((rows, width), F32),
        compiler_params=pltpu.CompilerParams(vmem_limit_bytes=4 * MIB),
        cost_estimate=pl.CostEstimate(
            flops=2 * rows * depth * width, bytes_accessed=2 * depth * width, transcendentals=0
        ),
        name="out_own",
    )(y, pinned(w))


def out_kernel(own_ref, z_ref, u_ref, a_ref, b_ref, c_ref, d_ref):
    rows, width = a_ref.shape
    step = 1024
    for at in range(0, width, step):
        cols = slice(at, at + step)
        total = own_ref[:, cols] + jnp.dot(
            z_ref[...], u_ref[:, cols], preferred_element_type=F32
        )
        for i, ref in enumerate((a_ref, b_ref, c_ref, d_ref)):
            ref[:, cols] = total[i * rows : (i + 1) * rows].astype(ref.dtype)


def out_rows(own, z, u):
    rows, width = own.shape
    send = jax.ShapeDtypeStruct((rows // 4, width), BF16)
    keep = jax.ShapeDtypeStruct((rows // 4, width), F32)
    return pl.pallas_call(
        out_kernel,
        in_specs=[VMEM] * 3,
        out_specs=[VMEM] * 4,
        out_shape=[send, keep, send, keep],
        compiler_params=pltpu.CompilerParams(vmem_limit_bytes=4 * MIB),
        cost_estimate=pl.CostEstimate(
            flops=2 * rows * z.shape[1] * width,
            bytes_accessed=2 * z.shape[1] * width,
            transcendentals=0,
        ),
        name="out_rows",
    )(pinned(own), z, pinned(u))


def paired_device(tokens, proj_weight, out_weight, head_gain, decay_rate):
    rows = tokens.shape[0]
    heads = decay_rate.shape[0]

    cuts = [proj_weight.shape[0] // STEP * part // 24 * STEP for part in (0, 10, 18)]
    w_other = hop(out_weight, CORE)
    first = hop(tokens, FIRST)
    outs = [
        jax.ShapeDtypeStruct(tokens.shape, tokens.dtype),
        pltpu.VMEM((8 * rows, 1), F32),
        pltpu.VMEM((1, 8 * rows), F32),
    ]
    *turned, passed, down, across = prep(0, cuts[1], proj_weight, [], tokens, outs, "prep_a")
    second = hop(passed, SECOND)
    beside = hop(tokens, CORE)
    (first,) = tie([first], [down])
    far = hop(first, SECOND)
    second_beside = hop(first, CORE)
    turned = prep(cuts[1], cuts[2], proj_weight, turned, tokens, [], "prep_b")
    kv, qg, x_all, k0, v0 = project_near(
        [passed, beside, first, second], cuts[2], proj_weight, *turned
    )
    first_beside = hop(second, CORE)
    (far,) = tie([far], [k0])
    far_beside = hop(far, CORE)
    x_all, q0 = early(x_all, qg)
    x_all, k1, v1, states = project_far(
        decay_rate, down, k0, v0, kv, x_all, [second_beside, first_beside, far, far_beside]
    )

    came = [
        lax.ppermute(states, "seq", [(i, (i + 1) % 4) for i in range(4)]),
        lax.ppermute(states, "seq", [(0, 2), (1, 3)]),
    ]
    came.append(lax.ppermute(states, "seq", [(0, 3)]))
    q1, g, w_own = gates(x_all, qg, out_weight)
    full = jax.ShapeDtypeStruct((8 * rows, heads * HD), F32)
    inner = small(inner_kernel, 1, full, "inner", decay_rate, down, across, q0, q1, k0, k1, v0, v1)
    split = jax.ShapeDtypeStruct((4 * rows, heads * HD), BF16)
    y, y_other = small(
        finish_kernel,
        1,
        [split, split],
        "finish",
        decay_rate, down, head_gain[None, :], inner, q0, q1, g, *came,
    )
    z = hop(y_other, CORE)
    a, b, c, d = out_rows(out_own(y, w_own), z, w_other)
    got_a = hop(a, SECOND)
    got_c = hop(c, SECOND)
    got_b = hop((b + got_a.astype(F32)).astype(BF16), FIRST)
    summed = lax.optimization_barrier(d + got_c.astype(F32))
    return (summed + got_b.astype(F32)).astype(BF16)


def solution(mesh):
    paired = mesh.shape["tp"] == 8 and mesh.shape["seq"] == 4
    return jax.shard_map(
        paired_device if paired else general_device,
        mesh=mesh,
        in_specs=(P(("seq", "tp"), None), P(None, None, "tp"), P("tp", None), P("tp"), P("tp")),
        out_specs=P(("seq", "tp"), None),
        check_vma=False,
    )
```

```python
import functools

import jax
import jax.numpy as jnp
from jax import lax
from jax.experimental import pallas as pl
from jax.experimental.pallas import tpu as pltpu
from jax.sharding import PartitionSpec as P

HD = 128
BLOCK = 256
F32, BF16 = jnp.float32, jnp.bfloat16
VMEM = pl.BlockSpec(memory_space=pltpu.VMEM)
SMEM = pl.BlockSpec(memory_space=pltpu.SMEM)
HBM = pl.BlockSpec(memory_space=pl.ANY)
MIB = 1 << 20


def entering(value, axis, combine, identity):
    count, position = (lax.axis_size(axis), lax.axis_index(axis))
    everything = jax.tree.map(
        lambda part, kind: lax.all_gather(part.astype(kind), axis),
        value,
        (jnp.bfloat16, jnp.bfloat16),
    )
    start = jax.tree.map(
        lambda part, zero: jnp.broadcast_to(jnp.asarray(zero, part.dtype), part.shape),
        value,
        identity,
    )

    def turn(k, before):
        reached = k < position
        new = combine(
            before, jax.tree.map(lambda part, own: part[k].astype(own.dtype), everything, value)
        )
        return jax.tree.map(lambda a, b: jnp.where(reached, a, b), new, before)

    return lax.fori_loop(0, count, turn, start)


def attend(q_head, k_head, v_head, rate, start_state):
    count = q_head.shape[0] // BLOCK
    place = jnp.arange(BLOCK).astype(jnp.float32)
    diff = place[:, None] - place[None, :]
    causal = jnp.where(diff >= 0, jnp.exp(-rate * jnp.maximum(diff, 0.0)), 0.0)
    in_decay = jnp.exp(-rate * (place + 1.0))
    out_decay = jnp.exp(-rate * (BLOCK - 1.0 - place))
    block_decay = jnp.exp(-rate * BLOCK)
    q_blocks = q_head.reshape(count, BLOCK, q_head.shape[1])
    k_blocks = k_head.reshape(count, BLOCK, k_head.shape[1])
    v_blocks = v_head.reshape(count, BLOCK, v_head.shape[1])

    def advance(state, block):
        q_blk, k_blk, v_blk = block
        scores = jnp.dot(q_blk, k_blk.T, preferred_element_type=jnp.float32)
        weighted = (scores * causal).astype(jnp.bfloat16)
        inner = jnp.dot(weighted, v_blk, preferred_element_type=jnp.float32)
        carried = (
            jnp.dot(q_blk.astype(jnp.float32), state, precision=lax.Precision.HIGHEST)
            * in_decay[:, None]
        )
        scaled = k_blk.astype(jnp.float32) * out_decay[:, None]
        update = jnp.dot(scaled.T, v_blk.astype(jnp.float32), precision=lax.Precision.HIGHEST)
        return (block_decay * state + update, inner + carried)

    final_state, outputs = lax.scan(advance, start_state, (q_blocks, k_blocks, v_blocks))
    return (outputs.reshape(q_head.shape[0], q_head.shape[1]), final_state)


def general_device(tokens, proj_weight, out_weight, head_gain, decay_rate):
    heads_here = decay_rate.shape[0]
    width = head_gain.shape[0]
    flat = proj_weight.reshape(proj_weight.shape[0], 4 * width)
    mixed = jnp.dot(
        lax.all_gather(tokens, "tp", axis=0, tiled=True), flat, preferred_element_type=jnp.float32
    )
    local_rows = mixed.shape[0]
    q_all = jax.nn.silu(mixed[:, :width]).astype(jnp.bfloat16).reshape(local_rows, heads_here, HD)
    k_all = (
        jax.nn.silu(mixed[:, width : 2 * width])
        .astype(jnp.bfloat16)
        .reshape(local_rows, heads_here, HD)
    )
    v_all = (
        jax.nn.silu(mixed[:, 2 * width : 3 * width])
        .astype(jnp.bfloat16)
        .reshape(local_rows, heads_here, HD)
    )
    gate = mixed[:, 3 * width :].reshape(local_rows, heads_here, HD)
    zero_state = jnp.zeros((HD, HD), jnp.float32)
    outputs, local_states = jax.vmap(attend, in_axes=(1, 1, 1, 0, None), out_axes=(1, 0))(
        q_all, k_all, v_all, decay_rate, zero_state
    )
    zero_states = jnp.zeros((heads_here, HD, HD), jnp.float32)
    span_decay = jnp.exp(-decay_rate * local_rows)

    def combine(earlier, later):
        return (later[1][:, None, None] * earlier[0] + later[0], earlier[1] * later[1])

    incoming, unused = entering(
        (local_states, span_decay), "seq", combine, (zero_states, jnp.ones_like(span_decay))
    )
    place = jnp.arange(local_rows).astype(jnp.float32)
    lift = jnp.exp(-decay_rate[None, :] * (place[:, None] + 1.0))
    extra = jnp.einsum(
        "thd,hde->the", q_all.astype(jnp.float32), incoming, precision=lax.Precision.HIGHEST
    )
    attn = outputs + extra * lift[:, :, None]
    square = jnp.mean(attn * attn, axis=-1, keepdims=True)
    normed = (
        attn
        * lax.rsqrt(square + 1e-06)
        * head_gain.reshape(heads_here, HD)[None]
        * jax.nn.sigmoid(gate)
    )
    joined = normed.astype(jnp.bfloat16).reshape(local_rows, width)
    return lax.psum_scatter(
        jnp.dot(joined, out_weight, preferred_element_type=jnp.float32).astype(jnp.bfloat16),
        "tp",
        scatter_dimension=0,
        tiled=True,
    )


CORE = [(i, i ^ 1) for i in range(8)]
FIRST = [(i, i ^ (4 if i & 1 else 2)) for i in range(8)]
SECOND = [(i, i ^ (2 if i & 1 else 4)) for i in range(8)]


def hop(value, pairs):
    return lax.ppermute(value, "tp", pairs)


STEP = 256
SLOTS = 8


def pinned(value):
    return pltpu.with_memory_space_constraint(value, pltpu.VMEM)


def in_hbm(value):
    return pltpu.with_memory_space_constraint(value, pltpu.HBM)


def chunks(first, count, w_hbm, buf, sem):
    slots, step = buf.shape[:2]

    def copy(i):
        return pltpu.make_async_copy(
            w_hbm.at[pl.ds(first + i * step, step)], buf.at[i % slots], sem.at[i % slots]
        )

    def arriving():
        for i in range(count):
            copy(i).wait()
            yield i, buf[i % slots]
            if i + slots < count:
                copy(i + slots).start()

    for i in range(min(slots, count)):
        copy(i).start()
    return arriving()


def turn(block, at, kv_ref, qg_ref):
    width = block.shape[2]
    turned = jnp.swapaxes(block, 0, 1)
    kv_ref[at, :width] = turned[1]
    kv_ref[at, width:] = turned[2]
    qg_ref[at, :width] = turned[0]
    qg_ref[at, width:] = turned[3]
    return turned


def slot_places(index, shape, axis):
    row = lax.broadcasted_iota(jnp.int32, shape, axis)
    part = shape[axis] // 8
    core = index & 1
    near = jnp.where(core == 0, 2, 4)
    far = 6 - near
    owners = (
        index,
        index ^ 1,
        index ^ near,
        index ^ far,
        index ^ 1 ^ far,
        index ^ 1 ^ near,
        index ^ 6,
        index ^ 7,
    )
    place = row
    for slot, owner in enumerate(owners):
        place = jnp.where(row // part == slot, row + (owner - slot) * part, place)
    return place.astype(F32)


def tie_kernel(*refs):
    pass


def tie(values, others):
    return pl.pallas_call(
        tie_kernel,
        in_specs=[HBM] * (len(values) + len(others)),
        out_specs=[HBM] * len(values),
        out_shape=[jax.ShapeDtypeStruct(v.shape, v.dtype) for v in values],
        input_output_aliases={i: i for i in range(len(values))},
        compiler_params=pltpu.CompilerParams(vmem_limit_bytes=MIB // 4),
        name="tie",
    )(*values, *others)


def prep_kernel(first, last, started, w_hbm, pass_ref, *refs):
    refs = refs[2 * started :]
    kv_ref, qg_ref, *outs = refs[:-3]
    buf, sem, pass_sem = refs[-3:]
    step = buf.shape[1]
    passing = []
    if outs:
        passing = [pltpu.make_async_copy(pass_ref, outs[0], pass_sem)]
    for copy in passing:
        copy.start()
    arriving = chunks(first, (last - first) // step, w_hbm, buf, sem)
    if outs:
        index = lax.axis_index("tp")
        for axis, ref in enumerate(outs[1:]):
            ref[...] = slot_places(index, ref.shape, axis)
    for i, block in arriving:
        turn(block, slice(first + i * step, first + (i + 1) * step), kv_ref, qg_ref)
    for copy in passing:
        copy.wait()


def prep(first, last, proj_weight, turned, passed, outs, name):
    depth, kinds, width = proj_weight.shape
    out = pltpu.VMEM((depth, 2 * width), BF16)
    slots = min(SLOTS, (last - first) // STEP)
    return pl.pallas_call(
        functools.partial(prep_kernel, first, last, bool(turned)),
        in_specs=[HBM, HBM] + [VMEM] * len(turned),
        out_specs=[VMEM] * (2 + len(outs)),
        out_shape=[out, out, *outs],
        scratch_shapes=[
            pltpu.VMEM((slots, STEP, kinds, width), BF16),
            pltpu.SemaphoreType.DMA((slots,)),
            pltpu.SemaphoreType.DMA,
        ],
        input_output_aliases={2 + i: i for i in range(len(turned))},
        compiler_params=pltpu.CompilerParams(vmem_limit_bytes=11 * MIB),
        cost_estimate=pl.CostEstimate(
            flops=0, bytes_accessed=4 * (last - first) * kinds * width, transcendentals=0
        ),
        name=name,
    )(in_hbm(proj_weight), in_hbm(passed), *map(pinned, turned))


def gather_rows(x_refs, x_all, at):
    for ref in x_refs:
        x_all[at : at + ref.shape[0], :] = ref[...]
        at += ref.shape[0]


def silu(mixed):
    return (mixed / (1.0 + jnp.exp(-mixed))).astype(BF16)


def near_kernel(n_rows, first, *refs):
    x_refs = refs[:n_rows]
    w_hbm, _, _, kv, qg, x_all, k_ref, v_ref, total, buf, sem = refs[n_rows:]
    step, (count, width) = buf.shape[1], k_ref.shape
    depth = kv.shape[0]
    arriving = chunks(first, (depth - first) // step, w_hbm, buf, sem)
    gather_rows(x_refs, x_all, 0)
    for i in range(2):
        total[i] = jnp.dot(
            x_all[:count, :first],
            kv[:first, i * width : (i + 1) * width],
            preferred_element_type=F32,
        )
    for c, block in arriving:
        at = first + c * step
        turned = turn(block, slice(at, at + step), kv, qg)
        for i in range(2):
            total[i] += jnp.dot(
                x_all[:count, at : at + step], turned[1 + i], preferred_element_type=F32
            )
    k_ref[...] = silu(total[0])
    v_ref[...] = silu(total[1])


def project_near(rows, first, proj_weight, kv, qg):
    count = sum(r.shape[0] for r in rows)
    depth, kinds, width = proj_weight.shape
    turned = pltpu.VMEM(kv.shape, BF16)
    half = pltpu.VMEM((count, width), BF16)
    slots = min(SLOTS, (depth - first) // STEP)
    return pl.pallas_call(
        functools.partial(near_kernel, len(rows), first),
        in_specs=[VMEM] * len(rows) + [HBM, VMEM, VMEM],
        out_specs=[VMEM] * 5,
        out_shape=[turned, turned, pltpu.VMEM((2 * count, depth), BF16), half, half],
        scratch_shapes=[
            pltpu.VMEM((2, count, width), F32),
            pltpu.VMEM((slots, STEP, kinds, width), BF16),
            pltpu.SemaphoreType.DMA((slots,)),
        ],
        input_output_aliases={len(rows) + 1: 0, len(rows) + 2: 1},
        compiler_params=pltpu.CompilerParams(vmem_limit_bytes=11 * MIB),
        cost_estimate=pl.CostEstimate(
            flops=2 * count * depth * kinds * width,
            bytes_accessed=4 * depth * kinds * width,
            transcendentals=0,
        ),
        name="project_near",
    )(*rows, in_hbm(proj_weight), pinned(kv), pinned(qg))


def far_kernel(n_rows, rate_ref, place_ref, k0, v0, kv, _, *refs):
    x_refs = refs[:n_rows]
    x_all, k_ref, v_ref, s_ref = refs[n_rows:]
    count, width = k_ref.shape
    gather_rows(x_refs, x_all, count)
    for i, ref in enumerate((k_ref, v_ref)):
        ref[...] = silu(
            jnp.dot(
                x_all[count:],
                kv[:, i * width : (i + 1) * width],
                preferred_element_type=F32,
            )
        )
    for h in range(s_ref.shape[0]):
        cols = slice(h * HD, (h + 1) * HD)
        fade = jnp.exp(-rate_ref[h] * (BLOCK - 1.0 - place_ref[...]))
        k = jnp.concatenate([k0[:, cols], k_ref[:, cols]], 0).astype(F32) * fade
        v = jnp.concatenate([v0[:, cols], v_ref[:, cols]], 0)
        s_ref[h] = lax.dot_general(
            k.astype(BF16), v, (((0,), (0,)), ((), ())), preferred_element_type=F32
        ).astype(BF16)


def project_far(rate, down, k0, v0, kv, x_all, rows):
    count = sum(r.shape[0] for r in rows)
    depth, width = rows[0].shape[1], k0.shape[1]
    half = pltpu.VMEM((count, width), BF16)
    return pl.pallas_call(
        functools.partial(far_kernel, len(rows)),
        in_specs=[SMEM] + [VMEM] * (5 + len(rows)),
        out_specs=[VMEM] * 4,
        out_shape=[
            pltpu.VMEM(x_all.shape, BF16),
            half,
            half,
            jax.ShapeDtypeStruct((rate.shape[0], HD, HD), BF16),
        ],
        input_output_aliases={5: 0},
        compiler_params=pltpu.CompilerParams(vmem_limit_bytes=2 * MIB),
        cost_estimate=pl.CostEstimate(
            flops=4 * count * depth * width, bytes_accessed=4 * depth * width, transcendentals=0
        ),
        name="project_far",
    )(rate, down, k0, v0, pinned(kv), pinned(x_all), *rows)


def block_decay(rate):
    return jnp.exp(jnp.full((HD, HD), -rate * BLOCK, F32))


def carry_kernel(rate_ref, own_ref, came_ref, _, o_ref):
    came = lax.axis_index("seq") > 0
    for h in range(o_ref.shape[0]):
        o_ref[h] = (
            own_ref[h].astype(F32)
            + jnp.where(came, block_decay(rate_ref[h]) * came_ref[h].astype(F32), 0.0)
        ).astype(BF16)


def early_kernel(_, qg, x_all, q_ref):
    count, width = q_ref.shape
    q_ref[...] = silu(jnp.dot(x_all[:count], qg[:, :width], preferred_element_type=F32))


def early(x_all, qg):
    count, depth = x_all.shape[0] // 2, x_all.shape[1]
    width = qg.shape[1] // 2

    return pl.pallas_call(
        early_kernel,
        in_specs=[VMEM, VMEM],
        out_specs=[VMEM, VMEM],
        out_shape=[pltpu.VMEM(x_all.shape, BF16), pltpu.VMEM((count, width), BF16)],
        input_output_aliases={0: 0},
        compiler_params=pltpu.CompilerParams(vmem_limit_bytes=2 * MIB),
        cost_estimate=pl.CostEstimate(
            flops=2 * count * depth * width, bytes_accessed=2 * depth * width, transcendentals=0
        ),
        name="early",
    )(pinned(x_all), pinned(qg))


def gates_kernel(x_all, qg, w_hbm, q_ref, g_ref, w_ref, sem):
    copy = pltpu.make_async_copy(w_hbm, w_ref, sem)
    copy.start()
    count, width = q_ref.shape
    q_ref[...] = silu(jnp.dot(x_all[count:], qg[:, :width], preferred_element_type=F32))
    mixed = jnp.dot(x_all[...], qg[:, width:], preferred_element_type=F32)
    g_ref[...] = 1.0 / (1.0 + jnp.exp(-mixed))
    copy.wait()


def gates(x_all, qg, w):
    count, depth = x_all.shape
    width = qg.shape[1] // 2
    return pl.pallas_call(
        gates_kernel,
        in_specs=[VMEM, VMEM, HBM],
        out_specs=[VMEM] * 3,
        out_shape=[
            pltpu.VMEM((count // 2, width), BF16),
            pltpu.VMEM((count, width), F32),
            pltpu.VMEM(w.shape, w.dtype),
        ],
        scratch_shapes=[pltpu.SemaphoreType.DMA],
        compiler_params=pltpu.CompilerParams(vmem_limit_bytes=2 * MIB),
        cost_estimate=pl.CostEstimate(
            flops=3 * count * depth * width, bytes_accessed=8 * depth * width, transcendentals=0
        ),
        name="gates",
    )(pinned(x_all), pinned(qg), in_hbm(w))


def inner_kernel(rate_ref, place_ref, across_ref, q0, q1, k0, k1, v0, v1, o_ref):
    diff = place_ref[...] - across_ref[...]
    seen = diff >= 0
    diff = jnp.maximum(diff, 0.0)
    for h in range(o_ref.shape[1] // HD):
        cols = slice(h * HD, (h + 1) * HD)
        q = jnp.concatenate([q0[:, cols], q1[:, cols]], 0)
        k = jnp.concatenate([k0[:, cols], k1[:, cols]], 0)
        v = jnp.concatenate([v0[:, cols], v1[:, cols]], 0)
        scores = lax.dot_general(q, k, (((1,), (1,)), ((), ())), preferred_element_type=F32)
        causal = jnp.where(seen, jnp.exp(-rate_ref[h] * diff), 0.0)
        o_ref[:, cols] = jnp.dot(
            (scores * causal).astype(BF16), v, preferred_element_type=F32
        )


TO_SUM = (3, 7, 1, 2, 5, 6, 0, 4)


def finish_kernel(rate_ref, place_ref, gain_ref, in_ref, q0, q1, g_ref, s1, s2, s3, y_ref, z_ref):
    part = in_ref.shape[0] // 8
    block = lax.axis_index("seq")
    for h in range(in_ref.shape[1] // HD):
        cols = slice(h * HD, (h + 1) * HD)
        rate = rate_ref[h]
        fade = block_decay(rate)
        state = jnp.where(block > 0, s1[h].astype(F32), 0.0) + fade * (
            jnp.where(block > 1, s2[h].astype(F32), 0.0)
            + fade * jnp.where(block > 2, s3[h].astype(F32), 0.0)
        )
        high = state.astype(BF16)
        low = (state - high.astype(F32)).astype(BF16)
        q = jnp.concatenate([q0[:, cols], q1[:, cols]], 0)
        extra = jnp.dot(q, high, preferred_element_type=F32) + jnp.dot(
            q, low, preferred_element_type=F32
        )
        attn = in_ref[:, cols] + extra * jnp.exp(-rate * (place_ref[...] + 1.0))
        square = jnp.mean(attn * attn, axis=-1, keepdims=True)
        y = (attn * lax.rsqrt(square + 1e-06) * gain_ref[:, cols] * g_ref[:, cols]).astype(BF16)
        for slot, to in enumerate(TO_SUM):
            to_ref, at = (y_ref, to) if to < 4 else (z_ref, to - 4)
            to_ref[at * part : (at + 1) * part, cols] = y[slot * part : (slot + 1) * part]


def small(kernel, n_smem, out, name, *args):
    return pl.pallas_call(
        kernel,
        in_specs=[SMEM] * n_smem + [VMEM] * (len(args) - n_smem),
        out_specs=jax.tree.map(lambda _: VMEM, out),
        out_shape=out,
        compiler_params=pltpu.CompilerParams(vmem_limit_bytes=3 * MIB),
        name=name,
    )(*args)


def out_own_kernel(y_ref, w_ref, o_ref):
    step = 1024
    for at in range(0, o_ref.shape[1], step):
        cols = slice(at, at + step)
        o_ref[:, cols] = jnp.dot(y_ref[...], w_ref[:, cols], preferred_element_type=F32)


def out_own(y, w):
    rows, depth = y.shape
    width = w.shape[1]
    return pl.pallas_call(
        out_own_kernel,
        in_specs=[VMEM] * 2,
        out_specs=VMEM,
        out_shape=pltpu.VMEM((rows, width), F32),
        compiler_params=pltpu.CompilerParams(vmem_limit_bytes=4 * MIB),
        cost_estimate=pl.CostEstimate(
            flops=2 * rows * depth * width, bytes_accessed=2 * depth * width, transcendentals=0
        ),
        name="out_own",
    )(y, pinned(w))


def out_kernel(own_ref, z_ref, u_ref, a_ref, b_ref, c_ref, d_ref):
    rows, width = a_ref.shape
    step = 1024
    for at in range(0, width, step):
        cols = slice(at, at + step)
        total = own_ref[:, cols] + jnp.dot(
            z_ref[...], u_ref[:, cols], preferred_element_type=F32
        )
        for i, ref in enumerate((a_ref, b_ref, c_ref, d_ref)):
            ref[:, cols] = total[i * rows : (i + 1) * rows].astype(ref.dtype)


def out_rows(own, z, u):
    rows, width = own.shape
    send = jax.ShapeDtypeStruct((rows // 4, width), BF16)
    keep = jax.ShapeDtypeStruct((rows // 4, width), F32)
    return pl.pallas_call(
        out_kernel,
        in_specs=[VMEM] * 3,
        out_specs=[VMEM] * 4,
        out_shape=[send, keep, send, keep],
        compiler_params=pltpu.CompilerParams(vmem_limit_bytes=4 * MIB),
        cost_estimate=pl.CostEstimate(
            flops=2 * rows * z.shape[1] * width,
            bytes_accessed=2 * z.shape[1] * width,
            transcendentals=0,
        ),
        name="out_rows",
    )(pinned(own), z, pinned(u))


def paired_device(tokens, proj_weight, out_weight, head_gain, decay_rate):
    rows = tokens.shape[0]
    heads = decay_rate.shape[0]

    cuts = [proj_weight.shape[0] // STEP * part // 24 * STEP for part in (0, 10, 19)]
    w_other = hop(out_weight, CORE)
    first = hop(tokens, FIRST)
    outs = [
        jax.ShapeDtypeStruct(tokens.shape, tokens.dtype),
        pltpu.VMEM((8 * rows, 1), F32),
        pltpu.VMEM((1, 8 * rows), F32),
    ]
    *turned, passed, down, across = prep(0, cuts[1], proj_weight, [], tokens, outs, "prep_a")
    second = hop(passed, SECOND)
    beside = hop(tokens, CORE)
    (first,) = tie([first], [down])
    far = hop(first, SECOND)
    second_beside = hop(first, CORE)
    turned = prep(cuts[1], cuts[2], proj_weight, turned, tokens, [], "prep_b")
    kv, qg, x_all, k0, v0 = project_near(
        [passed, beside, first, second], cuts[2], proj_weight, *turned
    )
    first_beside = hop(second, CORE)
    (far,) = tie([far], [k0])
    far_beside = hop(far, CORE)
    x_all, q0 = early(x_all, qg)
    x_all, k1, v1, states = project_far(
        decay_rate, down, k0, v0, kv, x_all, [second_beside, first_beside, far, far_beside]
    )

    came = [
        lax.ppermute(states, "seq", [(i, (i + 1) % 4) for i in range(4)]),
        lax.ppermute(states, "seq", [(0, 2), (1, 3)]),
    ]
    came.append(lax.ppermute(states, "seq", [(0, 3)]))
    q1, g, w_own = gates(x_all, qg, out_weight)
    full = jax.ShapeDtypeStruct((8 * rows, heads * HD), F32)
    inner = small(inner_kernel, 1, full, "inner", decay_rate, down, across, q0, q1, k0, k1, v0, v1)
    split = jax.ShapeDtypeStruct((4 * rows, heads * HD), BF16)
    y, y_other = small(
        finish_kernel,
        1,
        [split, split],
        "finish",
        decay_rate, down, head_gain[None, :], inner, q0, q1, g, *came,
    )
    z = hop(y_other, CORE)
    a, b, c, d = out_rows(out_own(y, w_own), z, w_other)
    got_a = hop(a, SECOND)
    got_c = hop(c, SECOND)
    got_b = hop((b + got_a.astype(F32)).astype(BF16), FIRST)
    summed = lax.optimization_barrier(d + got_c.astype(F32))
    return (summed + got_b.astype(F32)).astype(BF16)


def solution(mesh):
    paired = mesh.shape["tp"] == 8 and mesh.shape["seq"] == 4
    return jax.shard_map(
        paired_device if paired else general_device,
        mesh=mesh,
        in_specs=(P(("seq", "tp"), None), P(None, None, "tp"), P("tp", None), P("tp"), P("tp")),
        out_specs=P(("seq", "tp"), None),
        check_vma=False,
    )
```
